32 devices in a mesh: dp: 16 (over z, x, core), cent: 2 (over y).
Axes of the slice: x: 2, y: 2, z: 4, core: 2. Of those that a mesh axis runs over, the one named last changes fastest.
Arguments:
- vectors: bfloat16 [16384, 768], P('dp'), may hold values from -64 to 64
- centroids: bfloat16 [8192, 768], P('cent'), may hold values from -5 to 5
- prior_mass: float32 [8192], P('cent'), may hold values from 0.5 to 8
- assign: int32 [16384], P('dp'), may hold values from 0 to 8191, as said below
- owner_of: int32 [8192], replicated, may hold values from 0 to 15, as said below
- rotation: bfloat16 [768, 768], replicated, may hold values from -0.21875 to 0.21875
Outputs:
- new_centroids: float32 [2, 4096, 768], P('cent', 'dp')
- moments: float32 [16, 16, 768], P('dp', None, 'cent')
The draws below stay inside these ranges and needn't reach their ends.
Inputs may be any that keep to these rules, and one draw needn't show every extreme that they name: `assign`: of the 1024 vectors of each dp index, exactly 512 have their list in each block of 4096 consecutive lists; of those, at most 128 have lists of one owner, and for each block of lists one owner, the same for every dp index, receives exactly 128 from every dp index. `owner_of`: each owner holds exactly 256 lists of each block of 4096 consecutive lists.
All inputs are finite; a program needn't handle non-finite values.
Results may differ from the reference program's by a relative error of at most 0.0033.
Values may be sent and summed in bfloat16 or wider, within the bound.
No kernel may reach another device: no remote copies, remote signals or barrier semaphores. Data moves between devices by JAX's collectives and lax.ppermute only.
A program may use at most 64 MiB of HBM per device.

```python
import math
import jax
import jax.numpy as jnp
from jax import lax

D = 768
K = 8192
M = 48
TOK_DEV = 1024
N = 16384
KC = 4096
CAP = 128
N_DP = 16
N_CENT = 2


def centroid_table(key):
    base_key = jax.random.fold_in(key, 101)
    table = jnp.clip(jax.random.normal(base_key, (K, D), jnp.float32), -5.0, 5.0)
    return table.astype(jnp.bfloat16).astype(jnp.float32)


def draw_centroids(key, part):
    return centroid_table(key).astype(jnp.bfloat16)


def draw_vectors(key, part):
    key_list = jax.random.split(jax.random.fold_in(key, 202), 1)
    row_vals = jnp.clip(jax.random.normal(key_list[0], (N, D), jnp.float32), -6.0, 6.0)
    return row_vals.astype(jnp.bfloat16)


def routing_tables(key):
    base_key = jax.random.fold_in(key, 303)
    key_own, key_grade, key_full, key_pick, key_member, key_place = jax.random.split(base_key, 6)
    per_shard = TOK_DEV // N_CENT
    slot_total = N_DP * CAP
    perms = jax.vmap(lambda sub_key: jax.random.permutation(sub_key, KC))(jax.random.split(key_own, N_CENT)).astype(jnp.int32)
    owner_table = (perms % N_DP).reshape(K).astype(jnp.int32)
    inverse = jnp.argsort(perms, axis=1).astype(jnp.int32)
    quality_rank = jax.random.randint(key_grade, (N_CENT, N_DP), 0, 4)
    preferred_list = jax.random.randint(key_full, (N_CENT,), 0, N_DP)
    owner_span = jnp.arange(N_DP, dtype=jnp.int32)
    extra_reward = quality_rank * 256 + jnp.where(owner_span[None, :] == preferred_list[:, None], 2048, 0)
    slot_holder = jnp.arange(slot_total, dtype=jnp.int32) // CAP
    random_jitter = jax.random.randint(key_pick, (N_DP, N_CENT, slot_total), 0, 1024)
    merit_value = random_jitter + extra_reward[:, slot_holder][None, :, :]
    ranked = merit_value * 4096 + jnp.arange(slot_total, dtype=jnp.int32)[None, None, :]
    _, chosen = lax.top_k(ranked, per_shard)
    owner_ids = (chosen // CAP).astype(jnp.int32)
    member = jax.random.randint(key_member, (N_DP, N_CENT, per_shard), 0, KC // N_DP)
    shard_grid = jnp.broadcast_to(jnp.arange(N_CENT, dtype=jnp.int32)[None, :, None], owner_ids.shape)
    list_ids = shard_grid * KC + inverse[shard_grid, owner_ids + N_DP * member]
    flat_ids = list_ids.reshape(N_DP, TOK_DEV).astype(jnp.int32)
    orders = jax.vmap(lambda sub_key: jax.random.permutation(sub_key, TOK_DEV))(jax.random.split(key_place, N_DP))
    placed = jax.vmap(lambda spots, values: jnp.zeros((TOK_DEV,), jnp.int32).at[spots].set(values))(orders, flat_ids)
    return (owner_table, placed.reshape(N).astype(jnp.int32))


def draw_assign(key, part):
    return routing_tables(key)[1].astype(jnp.int32)


def draw_owner_of(key, part):
    return routing_tables(key)[0].astype(jnp.int32)


def shard_levels(rng, extent, shards, low, largest):
    loudness = 1.0
    for position, parts in shards:
        steps = jax.random.uniform(jax.random.fold_in(jax.random.fold_in(rng, 6), position), (parts,), jnp.float32, low / len(shards), largest / len(shards))
        loudness = loudness * jnp.repeat(jnp.exp(steps), extent[position] // parts).reshape((-1,) + (1,) * (len(extent) - 1 - position))
    return loudness


def gaussian(own_key, extent, width, bound, kind=jnp.bfloat16):
    result = width * jax.random.normal(own_key, extent, jnp.float32)
    return jnp.clip(result, min=-bound, max=bound).astype(kind)


def setup_inputs(seed: int = 0) -> dict:
    arg_keys = jax.random.split(jax.random.key(seed), 7)
    vectors = draw_vectors(jax.random.fold_in(arg_keys[6], 71), 0)
    centroids = draw_centroids(jax.random.fold_in(arg_keys[6], 71), 0)
    prior_mass = jnp.clip(jnp.exp(math.log(8.0) - 2.7725887 * jax.random.uniform(arg_keys[2], (K,), jnp.float32) ** shard_levels(arg_keys[2], (K,), ((0, 2),), -0.2, 0.2)), 0.5, 8.0)
    assign = draw_assign(jax.random.fold_in(arg_keys[6], 71), 0)
    owner_of = draw_owner_of(jax.random.fold_in(arg_keys[6], 71), 0)
    rotation = gaussian(arg_keys[5], (D, D), D ** -0.5, 0.21875)
    return dict(vectors=vectors, centroids=centroids, prior_mass=prior_mass, assign=assign, owner_of=owner_of, rotation=rotation)


def reference(vectors, centroids, prior_mass, assign, owner_of, rotation):
    inv_root = 1.0 / math.sqrt(D)
    cent_full = centroids.astype(jnp.float32)
    cent_square = lax.optimization_barrier(jnp.sum(cent_full * cent_full, axis=1))
    row_blocks = vectors.reshape(N_DP, TOK_DEV, D)

    def fold_block(running, row_block):
        sum_rows, soft_mass = running
        cross_dot = lax.dot_general(row_block, centroids, (((1,), (1,)), ((), ())), preferred_element_type=jnp.float32)
        scores = (2.0 * cross_dot - cent_square[None, :]) * inv_root
        peak_val = lax.optimization_barrier(jnp.max(scores, axis=1))
        exp_scores = jnp.exp(scores - peak_val[:, None])
        row_total = lax.optimization_barrier(jnp.sum(exp_scores, axis=1))
        member_prob = (exp_scores / row_total[:, None]).astype(jnp.bfloat16)
        sum_rows = sum_rows + lax.dot_general(member_prob, row_block, (((0,), (0,)), ((), ())), preferred_element_type=jnp.float32)
        soft_mass = soft_mass + lax.optimization_barrier(jnp.sum(member_prob.astype(jnp.float32), axis=0))
        return ((sum_rows, soft_mass), None)
    start_state = (jnp.zeros((K, D), jnp.float32), jnp.zeros((K,), jnp.float32))
    (sum_rows, soft_mass), _ = lax.scan(fold_block, start_state, row_blocks)
    updated = (prior_mass[:, None] * cent_full + sum_rows) / (prior_mass + soft_mass)[:, None]
    new_centroids = updated.reshape(N_CENT, KC, D)
    residual = (vectors.astype(jnp.float32) - cent_full[assign]).astype(jnp.bfloat16)
    rotated = jnp.dot(residual, rotation, preferred_element_type=jnp.float32).astype(jnp.bfloat16)
    owners = owner_of[assign]
    flat_rows = rotated.astype(jnp.float32).reshape(N, M, D // M)

    def owner_moments(owner_idx):
        weight = (owners == owner_idx).astype(jnp.float32)
        return jnp.einsum('r,rmi,rmj->imj', weight, flat_rows, flat_rows).reshape(D // M, D) / TOK_DEV
    moments = lax.map(owner_moments, jnp.arange(N_DP, dtype=jnp.int32))
    return (new_centroids, moments)
```

```python
import functools
import math

import jax
import jax.numpy as jnp
from jax import lax
from jax.experimental import pallas as pl
from jax.experimental.pallas import tpu as pltpu
from jax.sharding import PartitionSpec as P

M = 48
VMEM_LIMIT = 56 * 1024 * 1024
F32 = jnp.float32
BF16 = jnp.bfloat16


def params(steps=1):
    return pltpu.CompilerParams(
        dimension_semantics=("arbitrary",) * steps, vmem_limit_bytes=VMEM_LIMIT
    )


def dot(a, b, ca, cb):
    return lax.dot_general(a, b, (((ca,), (cb,)), ((), ())), preferred_element_type=F32)


def score_kernel(ids_ref, v_ref, c_ref, s_ref, st_ref, vt_ref, *, scale):
    step = pl.program_id(0)

    @pl.when(step == 0)
    def _():
        vt_ref[...] = v_ref[...].T
        st_ref[...] = jnp.zeros_like(st_ref)
        st_ref[0:1, :] = jnp.full((1, st_ref.shape[1]), -jnp.inf, F32)

    c = c_ref[0]
    c32 = c.astype(F32)
    square = jnp.sum(c32 * c32, axis=1, keepdims=True) * scale
    s = dot(c, vt_ref[...], 1, 0) * (2.0 * scale) - square
    s_ref[0] = s
    old_peak = st_ref[0:1, :]
    peak = jnp.maximum(old_peak, jnp.max(s, axis=0, keepdims=True))
    part = jnp.sum(jnp.exp2(s - peak), axis=0, keepdims=True)
    st_ref[1:2, :] = st_ref[1:2, :] * jnp.exp2(old_peak - peak) + part
    st_ref[0:1, :] = peak


def scores_of(ids, v, c_blocks, scale):
    n, (_, rows, width) = ids.shape[0], c_blocks.shape
    count = v.shape[0]
    return pl.pallas_call(
        functools.partial(score_kernel, scale=scale),
        grid_spec=pltpu.PrefetchScalarGridSpec(
            num_scalar_prefetch=1,
            grid=(n,),
            in_specs=[
                pl.BlockSpec((count, width), lambda i, ids: (0, 0)),
                pl.BlockSpec((1, rows, width), lambda i, ids: (ids[i], 0, 0)),
            ],
            out_specs=[
                pl.BlockSpec((1, rows, count), lambda i, ids: (i, 0, 0)),
                pl.BlockSpec((8, count), lambda i, ids: (0, 0)),
            ],
            scratch_shapes=[pltpu.VMEM((width, count), BF16)],
        ),
        out_shape=[
            jax.ShapeDtypeStruct((n, rows, count), F32),
            jax.ShapeDtypeStruct((8, count), F32),
        ],
        compiler_params=params(),
        cost_estimate=pl.CostEstimate(
            flops=2 * n * rows * width * count,
            bytes_accessed=4 * n * rows * count,
            transcendentals=n * rows * count,
        ),
        name="scores",
    )(ids, v, c_blocks)


def sums_kernel(s1_ref, s2_ref, st_ref, v1_ref, v2_ref, o_ref, m_ref):
    def resp(s_ref, row):
        peak, inverse = st_ref[row : row + 1, :], st_ref[row + 1 : row + 2, :]
        return (jnp.exp2(s_ref[0] - peak) * inverse).astype(BF16)

    r1, r2 = resp(s1_ref, 0), resp(s2_ref, 2)
    o_ref[0] = (dot(r1, v1_ref[...], 1, 0) + dot(r2, v2_ref[...], 1, 0)).astype(o_ref.dtype)
    both = r1.astype(F32) + r2.astype(F32)
    rows, count = both.shape
    lanes = 128 if count % 128 == 0 else count
    part = both[:, :lanes]
    for k in range(lanes, count, lanes):
        part = part + both[:, k : k + lanes]
    m_ref[0] = jnp.sum(part.T, axis=0, keepdims=True)


def sums_of(s1, s2, stats, v1, v2, first, n, out_dtype):
    _, rows, count = s1.shape
    width = v1.shape[1]
    score_spec = pl.BlockSpec((1, rows, count), lambda i: (first + i, 0, 0))
    v_spec = pl.BlockSpec((count, width), lambda i: (0, 0))
    return pl.pallas_call(
        sums_kernel,
        grid=(n,),
        in_specs=[score_spec, score_spec, pl.BlockSpec((4, count), lambda i: (0, 0)), v_spec, v_spec],
        out_specs=[
            pl.BlockSpec((1, rows, width), lambda i: (i, 0, 0)),
            pl.BlockSpec((1, 1, rows), lambda i: (i, 0, 0)),
        ],
        out_shape=[
            jax.ShapeDtypeStruct((n, rows, width), out_dtype),
            jax.ShapeDtypeStruct((n, 1, rows), F32),
        ],
        compiler_params=params(),
        cost_estimate=pl.CostEstimate(
            flops=4 * n * rows * width * count,
            bytes_accessed=8 * n * rows * count,
            transcendentals=2 * n * rows * count,
        ),
        name="sums",
    )(s1, s2, stats, v1, v2)


def residual_kernel(
    list_ref, v_ref, c_ref, owner_ref, rot_ref, r_ref, own_ref, picked_ref, ids_ref, acc_ref
):
    step = pl.program_id(0)
    per_shard, width = picked_ref.shape
    row_count = v_ref.shape[0]
    chunk = c_ref.shape[0]

    @pl.when(step == 0)
    def _():
        lists = list_ref[...]
        inside = lists >= 0
        upper = lax.broadcasted_iota(jnp.int32, (row_count, row_count), 0) <= (
            lax.broadcasted_iota(jnp.int32, (row_count, row_count), 1)
        )
        flags = jnp.broadcast_to(inside.astype(F32), (16, row_count)).astype(BF16)
        rank = dot(flags, upper.astype(F32).astype(BF16), 1, 0)[0:1, :].astype(jnp.int32)
        slot = jnp.where(inside, rank - 1, -1)
        pick = slot == lax.broadcasted_iota(jnp.int32, (per_shard, row_count), 0)
        picked_ref[...] = dot(pick.astype(F32).astype(BF16), v_ref[...], 1, 0)
        ids = jnp.sum(jnp.where(pick, lists, 0).astype(F32), axis=1, keepdims=True)
        ids_ref[...] = jnp.broadcast_to(ids.astype(jnp.int32), ids_ref.shape)
        acc_ref[...] = jnp.zeros_like(acc_ref)
        own_ref[...] = jnp.zeros_like(own_ref)

    ids = ids_ref[:, 0:1]
    here = ids == lax.broadcasted_iota(jnp.int32, (per_shard, chunk), 1) + step * chunk
    acc_ref[...] += dot(here.astype(F32).astype(BF16), c_ref[...], 1, 0)
    owner = jnp.where(here, owner_ref[...], 0).astype(F32)
    own_ref[...] += jnp.broadcast_to(jnp.sum(owner, axis=1, keepdims=True), own_ref.shape)

    @pl.when(step == pl.num_programs(0) - 1)
    def _():
        residual = (picked_ref[...] - acc_ref[...]).astype(BF16)
        r_ref[...] = dot(residual, rot_ref[...], 1, 0).astype(BF16)


def rotated_residuals(lists, v, centroids, owner, rotation, per_shard):
    row_count, width = v.shape
    total = centroids.shape[0]
    chunk = min(512, total)
    n = total // chunk
    fixed = lambda i: (0, 0)
    return pl.pallas_call(
        residual_kernel,
        grid=(n,),
        in_specs=[
            pl.BlockSpec((1, row_count), fixed),
            pl.BlockSpec((row_count, width), fixed),
            pl.BlockSpec((chunk, width), lambda i: (i, 0)),
            pl.BlockSpec((1, chunk), lambda i: (0, i)),
            pl.BlockSpec((width, width), fixed),
        ],
        out_specs=[
            pl.BlockSpec((per_shard, width), fixed),
            pl.BlockSpec((per_shard, 128), fixed),
        ],
        out_shape=[
            jax.ShapeDtypeStruct((per_shard, width), BF16),
            jax.ShapeDtypeStruct((per_shard, 128), F32),
        ],
        scratch_shapes=[
            pltpu.VMEM((per_shard, width), F32),
            pltpu.VMEM((per_shard, 128), jnp.int32),
            pltpu.VMEM((per_shard, width), F32),
        ],
        compiler_params=params(),
        cost_estimate=pl.CostEstimate(
            flops=2 * per_shard * width * (total + row_count + width),
            bytes_accessed=2 * total * width,
            transcendentals=0,
        ),
        name="residuals",
    )(lists, v, centroids, owner, rotation)


def moment_kernel(ids_ref, r_ref, own_ref, o_ref, *, sub):
    owners = o_ref.shape[0]
    rows, tile = r_ref.shape
    turned = r_ref[...].T
    own = own_ref[...].T[0:1, :]
    fold = tile // sub
    diagonal = (lax.broadcasted_iota(jnp.int32, (tile, tile), 0) // sub) == (
        lax.broadcasted_iota(jnp.int32, (tile, tile), 1) // sub
    )

    for place in range(owners):
        hit = own == ids_ref[place].astype(F32)
        masked = jnp.where(hit, turned.astype(F32), 0.0).astype(BF16)
        gram = jnp.where(diagonal, dot(masked, r_ref[...], 1, 0), 0.0)
        o_ref[place] = jnp.sum(gram.reshape(fold, sub, tile), axis=0)


def owner_moments(ids, rotated, own, sub):
    rows, width = rotated.shape
    owners = ids.shape[0]
    tile = 256 if width % 256 == 0 else width
    return pl.pallas_call(
        functools.partial(moment_kernel, sub=sub),
        grid_spec=pltpu.PrefetchScalarGridSpec(
            num_scalar_prefetch=1,
            grid=(width // tile,),
            in_specs=[
                pl.BlockSpec((rows, tile), lambda i, ids: (0, i)),
                pl.BlockSpec((rows, 128), lambda i, ids: (0, 0)),
            ],
            out_specs=pl.BlockSpec((owners, sub, tile), lambda i, ids: (0, 0, i)),
        ),
        out_shape=jax.ShapeDtypeStruct((owners, sub, width), F32),
        compiler_params=params(),
        cost_estimate=pl.CostEstimate(
            flops=2 * owners * rows * tile * width, bytes_accessed=4 * owners * sub * width, transcendentals=0
        ),
        name="moments",
    )(ids, rotated, own)


def flip(array, axis, mask):
    size = lax.axis_size(axis)
    return lax.ppermute(array, axis, [(i, i ^ mask) for i in range(size)])


def merge(a, b):
    top = jnp.maximum(a[0], b[0])
    return jnp.stack([top, a[1] * jnp.exp2(a[0] - top) + b[1] * jnp.exp2(b[0] - top)])


def reverse_bits(value, bits):
    return sum(((value >> k) & 1) << (bits - 1 - k) for k in range(bits))


def body(vectors, centroids, prior_mass, assign, owner_of, rotation):
    row_count, width = vectors.shape
    shard_rows = centroids.shape[0]
    cent_count, dp_count = lax.axis_size("cent"), lax.axis_size("dp")
    cent_pos, dp_pos = lax.axis_index("cent"), lax.axis_index("dp")
    bits = dp_count.bit_length() - 1
    levels = bits - 1
    block = shard_rows // dp_count
    scale = math.log2(math.e) / math.sqrt(width)

    half = dp_count // 4
    places = [1 + 2 * k for k in reversed(range(half))] + [2 * k for k in reversed(range(half))]
    ids = dp_pos ^ (2 * jnp.array(places, jnp.int32))
    c_blocks = centroids.reshape(dp_count, block, width)

    other = flip(vectors, "dp", 1)
    s1, st1 = scores_of(ids, vectors, c_blocks, scale)
    s2, st2 = scores_of(ids, other, c_blocks, scale)
    mine = jnp.concatenate([st1[0:2], st2[0:2]])
    theirs = flip(mine, "dp", 1)
    stats = jnp.concatenate([merge(mine[0:2], theirs[2:4]), merge(mine[2:4], theirs[0:2])])
    step = 1
    while step < cent_count:
        far = flip(stats, "cent", step)
        stats = jnp.concatenate([merge(stats[0:2], far[0:2]), merge(stats[2:4], far[2:4])])
        step *= 2
    stats = jnp.stack([stats[0], 1.0 / stats[1], stats[2], 1.0 / stats[3]])

    lists = jnp.where(assign // shard_rows == cent_pos, assign - cent_pos * shard_rows, -1)
    owner = lax.dynamic_slice_in_dim(owner_of, cent_pos * shard_rows, shard_rows, 0)
    rotated, own = rotated_residuals(
        lists[None], vectors, centroids, owner[None], rotation, row_count // cent_count
    )
    order = jnp.array([reverse_bits(k, bits) for k in range(dp_count)], jnp.int32)
    moments = owner_moments(dp_pos ^ order, rotated, own, width // M)

    parts, masses = {}, {}
    cuts = [(0, 1, BF16), (1, half - 1, BF16), (half, half, F32)]
    for first, n, kind in cuts:
        got, mass = sums_of(s1, s2, stats, vectors, other, first, n, kind)
        for k in range(n):
            parts[places[first + k]] = got[k]
            masses[places[first + k]] = mass[k]


    held = {}
    for place in places[:half]:
        held[place ^ 1] = parts[place ^ 1] + flip(parts[place], "dp", 2).astype(F32)
    for level in range(1, levels):
        bit = 1 << level
        sent = sorted((p for p in held if p & bit), reverse=True)
        for p in sent:
            came = flip(held.pop(p).astype(BF16), "dp", 2 * bit)
            held[p ^ bit] = held[p ^ bit] + came.astype(F32)
    own_sums = held[0]

    mass = jnp.concatenate([masses[reverse_bits(k, levels)] for k in range(2 * half)])
    for level in range(levels):
        n = mass.shape[0] // 2
        mass = mass[:n] + flip(mass[n:], "dp", 2 << level)
    own_mass = mass[0]

    n = dp_count // 2
    moments = moments[:n] + flip(moments[n:], "dp", 1)
    if cent_count == 2:
        near = width // 2
        mine = lax.dynamic_slice_in_dim(moments, cent_pos * near, near, 2)
        far = lax.dynamic_slice_in_dim(moments, (1 - cent_pos) * near, near, 2)
        moments = mine + flip(far, "cent", 1)
    else:
        moments = lax.psum_scatter(moments, "cent", scatter_dimension=2, tiled=True)
    for level in range(levels):
        n = moments.shape[0] // 2
        moments = moments[:n] + flip(moments[n:], "dp", 2 << level)
    moments = moments / row_count

    own_cent = lax.dynamic_slice_in_dim(centroids, dp_pos * block, block, 0).astype(F32)
    own_prior = lax.dynamic_slice_in_dim(prior_mass, dp_pos * block, block, 0)
    updated = (own_prior[:, None] * own_cent + own_sums) / (own_prior + own_mass)[:, None]
    return (updated[None], moments)


def solution(mesh):
    return jax.shard_map(
        body,
        mesh=mesh,
        in_specs=(P("dp", None), P("cent", None), P("cent"), P("dp"), P(), P()),
        out_specs=(P("cent", "dp", None), P("dp", None, "cent")),
        check_vma=False,
    )
```

```python
import functools
import math

import jax
import jax.numpy as jnp
from jax import lax
from jax.experimental import pallas as pl
from jax.experimental.pallas import tpu as pltpu
from jax.sharding import PartitionSpec as P

M = 48
CHUNK = 256
F32 = jnp.float32
BF16 = jnp.bfloat16
HBM = pl.BlockSpec(memory_space=pltpu.HBM)
VMEM = pl.BlockSpec(memory_space=pltpu.VMEM)
ANY = pl.BlockSpec(memory_space=pl.ANY)


def in_hbm(x):
    return pltpu.with_memory_space_constraint(x, pltpu.HBM)


def in_vmem(x):
    return pltpu.with_memory_space_constraint(x, pltpu.VMEM)


def params(mib):
    return pltpu.CompilerParams(vmem_limit_bytes=mib << 20)


def cost(flops, moved=0, exps=0):
    return pl.CostEstimate(flops=1024, bytes_accessed=1024, transcendentals=0)


def dot(a, b, ca, cb):
    return lax.dot_general(a, b, (((ca,), (cb,)), ((), ())), preferred_element_type=F32)


def reverse_bits(value, bits):
    return sum(((value >> k) & 1) << (bits - 1 - k) for k in range(bits))


def piece_order(levels, block):
    rest = levels - 3
    inner = [reverse_bits(k, rest) if rest else 0 for k in range(1 << rest)]
    order, pieces = [], {}
    for first, kind in ((1, "send"), (0, "keep")):
        for second, third in ((1, 1), (0, 1), (1, 0), (0, 0)):
            pieces[kind + str(second + 2 * third)] = (len(order) * block, len(inner) * block)
            order += [first + 2 * (second + 2 * third + 4 * k) for k in inner]
    return tuple(order), pieces


def swapped(place):
    return (place & ~3) | ((place & 1) << 1) | ((place >> 1) & 1)


def masks(level):
    return tuple(2 * p for p in ((1 << level), swapped(1 << level)))


def block_at(place, core):
    return lax.axis_index("dp") ^ jnp.where(core == 0, 2 * place, 2 * swapped(place))


def this_core():
    return lax.rem(lax.axis_index("dp"), 2)


def score_chunks(c_ref, v_ref, s_ref, scale, ready=None):
    def product(k):
        return dot(c_ref[k : k + CHUNK], v_ref[...], 1, 1)

    chunks = range(0, c_ref.shape[0], CHUNK)
    peak = None
    ahead = product(0)
    if ready is not None:
        ready()
    for place, k in enumerate(chunks):
        now = ahead
        if place + 1 < len(chunks):
            ahead = product(chunks[place + 1])
        c = c_ref[k : k + CHUNK].astype(F32)
        s = now * (2.0 * scale) - jnp.sum(c * c, axis=1, keepdims=True) * scale
        s_ref[k : k + CHUNK] = s
        top = jnp.max(s, axis=0, keepdims=True)
        if peak is None:
            peak, total = top, jnp.sum(jnp.exp2(s - top), axis=0, keepdims=True)
        else:
            top = jnp.maximum(peak, top)
            total = total * jnp.exp2(peak - top) + jnp.sum(jnp.exp2(s - top), axis=0, keepdims=True)
            peak = top
    return peak, total


def first_scores_kernel(v_ref, c_ref, s_ref, st_ref, ch_ref, vh_ref, v_sem, c_sem, *, places, scale):
    rows = ch_ref.shape[0] // len(places)
    core = this_core()
    copies = [
        pltpu.make_async_copy(c_ref.at[block_at(p, core)], ch_ref.at[pl.ds(k * rows, rows)], c_sem.at[k])
        for k, p in enumerate(places)
    ]
    whole = pltpu.make_async_copy(v_ref, vh_ref, v_sem)
    early = CHUNK // rows
    whole.start()
    for copy in copies:
        copy.start()
    for copy in copies[:early]:
        copy.wait()
    whole.wait()

    def rest():
        for copy in copies[early:]:
            copy.wait()

    peak, total = score_chunks(ch_ref, vh_ref, s_ref, scale, rest)
    st_ref[0:1, :] = peak
    st_ref[1:2, :] = total


def first_scores(v, c_blocks, places, scale):
    _, block, width = c_blocks.shape
    count, held = v.shape[0], len(places) * block
    return pl.pallas_call(
        functools.partial(first_scores_kernel, places=places, scale=scale),
        in_specs=[HBM, HBM],
        out_specs=[VMEM] * 4,
        out_shape=[
            pltpu.VMEM((held, count), F32),
            pltpu.VMEM((2, count), F32),
            pltpu.VMEM((held, width), BF16),
            pltpu.VMEM((count, width), BF16),
        ],
        scratch_shapes=[pltpu.SemaphoreType.DMA, pltpu.SemaphoreType.DMA((len(places),))],
        compiler_params=params(8),
        cost_estimate=cost(2 * held * width * count, 4 * held * width, held * count),
        name="first_scores",
    )(in_hbm(v), in_hbm(c_blocks))


def second_scores_kernel(v_ref, ch_ref, st_ref, s_ref, both_ref, *, scale):
    peak, total = score_chunks(ch_ref, v_ref, s_ref, scale)
    both_ref[0:2, :] = st_ref[...]
    both_ref[2:3, :] = peak
    both_ref[3:4, :] = total


def second_scores(v, c_half, stats, scale):
    held, width = c_half.shape
    count = v.shape[0]
    return pl.pallas_call(
        functools.partial(second_scores_kernel, scale=scale),
        in_specs=[VMEM, VMEM, VMEM],
        out_specs=[VMEM] * 2,
        out_shape=[pltpu.VMEM((held, count), F32), jax.ShapeDtypeStruct((4, count), F32)],
        compiler_params=params(8),
        cost_estimate=cost(2 * held * width * count, 0, held * count),
        name="second_scores",
    )(in_vmem(v), in_vmem(c_half), in_vmem(stats))


def merged(a, b):
    top = jnp.maximum(a[0], b[0])
    return top, a[1] * jnp.exp2(a[0] - top) + b[1] * jnp.exp2(b[0] - top)


def pair(ref, row):
    return ref[row : row + 1, :], ref[row + 1 : row + 2, :]


def merge_kernel(a_ref, b_ref, _, o_ref, *, swap):
    for row in (0, 2):
        top, total = merged(pair(a_ref, row), pair(b_ref, 2 - row if swap else row))
        o_ref[row : row + 1, :] = top
        o_ref[row + 1 : row + 2, :] = total


def merge(a, b, token, swap):
    return pl.pallas_call(
        functools.partial(merge_kernel, swap=swap),
        in_specs=[VMEM, VMEM, ANY],
        out_specs=VMEM,
        out_shape=jax.ShapeDtypeStruct(a.shape, F32),
        compiler_params=params(2),
        cost_estimate=cost(8 * a.size),
        name="merge",
    )(a, b, token)


def sums_kernel(s1_ref, s2_ref, near_ref, far_ref, v1_ref, v2_ref, old_ref, _, *refs, which, sends, rank):
    n = len(which)
    outs, mass_ref, sem = refs[:n], refs[n], refs[-1]
    stages = refs[n + 1 : n + 1 + sends] + outs[sends:]
    mass_ref[...] = old_ref[...]
    core = this_core()
    stats = []
    for row in (0, 2):
        top, total = merged(pair(near_ref, row), pair(far_ref, row))
        stats.append((top, 1.0 / total))

    def resp(k, size):
        rows = slice(k, k + size)
        return [
            (jnp.exp2(ref[rows, :] - top) * inverse).astype(BF16)
            for ref, (top, inverse) in zip((s1_ref, s2_ref), stats)
        ]

    work = [
        (place, k, start + k, min(CHUNK, size))
        for place, (start, size) in enumerate(which)
        for k in range(0, size, min(CHUNK, size))
    ]
    copies = []
    ahead = resp(work[0][2], work[0][3])
    for turn, (place, inside, k, step) in enumerate(work):
        r1, r2 = ahead
        if turn + 1 < len(work):
            ahead = resp(*work[turn + 1][2:])
        total = dot(r1, v1_ref[...], 1, 0) + dot(r2, v2_ref[...], 1, 0)
        stages[place][inside : inside + step] = total.astype(stages[place].dtype)
        both = r1.astype(F32) + r2.astype(F32)
        part = both[:, :128]
        for lane in range(128, both.shape[1], 128):
            part = part + both[:, lane : lane + 128]
        mass = jnp.sum(part.T, axis=0, keepdims=True)
        block = mass_ref.shape[1]
        for low in range(0, step, block):
            rows = rank[(k + low) // block]
            mass_ref[pl.ds(jnp.where(core == 0, *rows), 1), :] = mass[:, low : low + block]
        if inside + step == which[place][1] and place < sends:
            copy = pltpu.make_async_copy(stages[place], outs[place], sem.at[place])
            copy.start()
            copies.append(copy)
    for copy in copies:
        copy.wait()


def sums_of(s1, s2, near, far, v1, v2, old, which, sends, rank, token):
    count, width = v1.shape
    rows = [size for _, size in which]
    return pl.pallas_call(
        functools.partial(sums_kernel, which=which, sends=sends, rank=rank),
        in_specs=[VMEM] * 7 + [ANY],
        out_specs=[HBM] * sends + [VMEM] * (len(which) - sends + 1),
        out_shape=[pltpu.HBM((size, width), BF16) for size in rows[:sends]]
        + [pltpu.VMEM((size, width), F32) for size in rows[sends:]]
        + [jax.ShapeDtypeStruct(old.shape, F32)],
        scratch_shapes=[pltpu.VMEM((size, width), BF16) for size in rows[:sends]]
        + [pltpu.SemaphoreType.DMA((sends,))],
        compiler_params=params(14),
        cost_estimate=cost(0),
        name="sums",
    )(in_vmem(s1), in_vmem(s2), near, far, in_vmem(v1), in_vmem(v2), old, token)


def pick_kernel(assign_ref, v_ref, _, picked_ref, ids_ref, *, total):
    per_shard = picked_ref.shape[0]
    row_count = v_ref.shape[0]
    lists = assign_ref[...] - lax.axis_index("cent") * total
    inside = jnp.logical_and(lists >= 0, lists < total)
    upper = lax.broadcasted_iota(jnp.int32, (row_count, row_count), 0) <= (
        lax.broadcasted_iota(jnp.int32, (row_count, row_count), 1)
    )
    flags = jnp.broadcast_to(inside.astype(F32), (16, row_count)).astype(BF16)
    rank = dot(flags, upper.astype(F32).astype(BF16), 1, 0)[0:1, :].astype(jnp.int32)
    slot = jnp.where(inside, rank - 1, -1)
    pick = slot == lax.broadcasted_iota(jnp.int32, (per_shard, row_count), 0)
    picked_ref[...] = dot(pick.astype(F32).astype(BF16), v_ref[...], 1, 0).astype(BF16)
    ids = jnp.sum(jnp.where(pick, lists, 0).astype(F32), axis=1, keepdims=True)
    ids_ref[...] = jnp.broadcast_to(ids.astype(jnp.int32), ids_ref.shape)


def picked_rows(assign, v, token, per_shard, total):
    width = v.shape[1]
    return pl.pallas_call(
        functools.partial(pick_kernel, total=total),
        in_specs=[VMEM, VMEM, ANY],
        out_specs=[VMEM, VMEM],
        out_shape=[pltpu.VMEM((per_shard, width), BF16), pltpu.VMEM((per_shard, 128), jnp.int32)],
        compiler_params=params(8),
        cost_estimate=cost(0),
        name="picked",
    )(assign, in_vmem(v), token)


def residual_kernel(
    picked_ref, ids_ref, near_ref, c_ref, owner_ref, rot_ref, _, r_ref, own_ref, far_ref, sem, *, places
):
    held, width = near_ref.shape
    total = 2 * held
    block = held // len(places)
    per_shard = r_ref.shape[0]
    core, cent_pos = this_core(), lax.axis_index("cent")
    copies = [
        pltpu.make_async_copy(c_ref.at[block_at(p, core) ^ 1], far_ref.at[pl.ds(k * block, block)], sem.at[k])
        for k, p in enumerate(places)
    ]
    for copy in copies:
        copy.start()
    ids = ids_ref[:, 0:1]
    chunk = min(1024, held)
    lane_ids = lax.broadcasted_iota(jnp.int32, (1, chunk), 1)

    def one_hot(k, other):
        here_ids = lane_ids
        for low in range(0, chunk, block):
            first = (block_at(places[(k + low) // block], core) ^ other) * block
            in_block = jnp.logical_and(lane_ids >= low, lane_ids < low + block)
            here_ids = jnp.where(in_block, lane_ids - low + first, here_ids)
        return (ids == here_ids).astype(F32).astype(BF16)

    lists = ids + cent_pos * total
    high = (lists // 128 == lax.broadcasted_iota(jnp.int32, (1, owner_ref.shape[0]), 1)).astype(F32)
    table = dot(high.astype(BF16), owner_ref[...].astype(F32).astype(BF16), 1, 0)
    low = lists % 128 == lax.broadcasted_iota(jnp.int32, (1, 128), 1)
    own = jnp.sum(jnp.where(low, table, 0.0), axis=1, keepdims=True)
    own_ref[...] = jnp.broadcast_to(own, own_ref.shape)
    gathered = jnp.zeros((per_shard, width), F32)
    for other, half_ref in enumerate((near_ref, far_ref)):
        if other:
            for copy in copies:
                copy.wait()
        for k in range(0, held, chunk):
            gathered = gathered + dot(one_hot(k, other), half_ref[k : k + chunk], 1, 0)
    residual = (picked_ref[...].astype(F32) - gathered).astype(BF16)
    r_ref[...] = dot(residual, rot_ref[...], 1, 0).astype(BF16)


def rotated_residuals(picked, ids, c_half, c_blocks, owner, rotation, token, places):
    per_shard, width = picked.shape
    held = c_half.shape[0]
    return pl.pallas_call(
        functools.partial(residual_kernel, places=places),
        in_specs=[VMEM] * 3 + [HBM] + [VMEM] * 2 + [ANY],
        out_specs=[VMEM, VMEM],
        out_shape=[
            pltpu.VMEM((per_shard, width), BF16),
            pltpu.VMEM((per_shard, 128), F32),
        ],
        scratch_shapes=[pltpu.VMEM((held, width), BF16), pltpu.SemaphoreType.DMA((len(places),))],
        compiler_params=params(14),
        cost_estimate=cost(0),
        name="residuals",
    )(in_vmem(picked), in_vmem(ids), in_vmem(c_half), in_hbm(c_blocks), owner, rotation, token)


def moment_kernel(r_ref, own_ref, _, __, ___, keep_ref, send_ref, all_ref, *, sub, order):
    rows, width = r_ref.shape
    half = len(order)
    tile = 256 if width % 256 == 0 else width
    own = own_ref[...].T[0:1, :]
    diagonal = (lax.broadcasted_iota(jnp.int32, (tile, tile), 0) // sub) == (
        lax.broadcasted_iota(jnp.int32, (tile, tile), 1) // sub
    )
    dp_pos = lax.axis_index("dp")
    owners = [dp_pos ^ (2 * p) for p in order] + [dp_pos ^ (2 * p + 1) for p in order]
    hits = [(own == owner.astype(F32)).astype(F32).astype(BF16) for owner in owners]
    for t in range(0, width, tile):
        r = r_ref[:, t : t + tile]
        turned = r.T
        for place, hit in enumerate(hits):
            gram = jnp.where(diagonal, dot(turned * hit, r, 1, 0), 0.0)
            all_ref[place, :, t : t + tile] = jnp.sum(gram.reshape(tile // sub, sub, tile), axis=0)
    keep_ref[...] = all_ref[:half]
    send_ref[...] = all_ref[half:].astype(send_ref.dtype)


def owner_moments(order, rotated, own, token, s1, s2, sub):
    rows, width = rotated.shape
    half = len(order)
    shape = (half, sub, width)
    return pl.pallas_call(
        functools.partial(moment_kernel, sub=sub, order=order),
        in_specs=[VMEM, VMEM, ANY, VMEM, VMEM],
        out_specs=[VMEM] * 2,
        out_shape=[jax.ShapeDtypeStruct(shape, F32), jax.ShapeDtypeStruct(shape, BF16)],
        scratch_shapes=[pltpu.VMEM((2 * half, sub, width), F32)],
        compiler_params=params(8),
        cost_estimate=cost(0),
        name="moments",
    )(in_vmem(rotated), in_vmem(own), token, in_vmem(s1), in_vmem(s2))


def side_kernel(a_ref, b_ref, _, mine_ref, theirs_ref, all_ref):
    all_ref[...] = a_ref[...] + b_ref[...].astype(F32)
    size = mine_ref.shape[2]
    cent_pos = lax.axis_index("cent")
    for ref, side in ((mine_ref, cent_pos), (theirs_ref, 1 - cent_pos)):
        ref[...] = all_ref[:, :, pl.ds(pl.multiple_of(side * size, 128), size)]


def sides(a, b, token):
    n, sub, width = a.shape
    return pl.pallas_call(
        side_kernel,
        in_specs=[VMEM, VMEM, ANY],
        out_specs=[VMEM] * 2,
        out_shape=[jax.ShapeDtypeStruct((n, sub, width // 2), F32)] * 2,
        scratch_shapes=[pltpu.VMEM(a.shape, F32)],
        compiler_params=params(6),
        cost_estimate=cost(0),
        name="sides",
    )(a, b, token)


def pack_kernel(*refs, n):
    parts, mass_ref, outs = refs[:n], refs[n], refs[n + 2 :]
    total = parts[0][...]
    for part in parts[1:]:
        total = total + part[...]
    sub, width = total.shape[1:]
    block = mass_ref.shape[1]
    size = outs[0].shape[0]
    for k, ref in enumerate(outs):
        ref[:, :sub, :] = total[k * size : (k + 1) * size]
        ref[:, sub:, :] = jnp.zeros((size, ref.shape[1] - sub, width), F32)
        for place in range(size):
            row = k * size + place
            ref[place, sub : sub + 1, :block] = mass_ref[row : row + 1, :]


def packed(parts, mass, token):
    n, sub, width = parts[0].shape
    return pl.pallas_call(
        functools.partial(pack_kernel, n=len(parts)),
        in_specs=[VMEM] * (len(parts) + 1) + [ANY],
        out_specs=[VMEM] * 2,
        out_shape=[jax.ShapeDtypeStruct((n // 2, sub + 8, width), F32)] * 2,
        compiler_params=params(6),
        cost_estimate=cost(0),
        name="packed",
    )(*parts, mass, token)


def halves_kernel(*refs, n):
    total = refs[0][...]
    for part in refs[1:n]:
        total = total + part[...]
    size = total.shape[0] // 2
    refs[n + 1][...] = total[:size]
    refs[n + 2][...] = total[size:]


def halves(parts, token):
    n, rows, width = parts[0].shape
    return pl.pallas_call(
        functools.partial(halves_kernel, n=len(parts)),
        in_specs=[VMEM] * len(parts) + [ANY],
        out_specs=[VMEM] * 2,
        out_shape=[jax.ShapeDtypeStruct((n // 2, rows, width), F32)] * 2,
        compiler_params=params(4),
        cost_estimate=cost(0),
        name="halves",
    )(*parts, token)


def flip(array, axis, mask):
    size = lax.axis_size(axis)
    return lax.ppermute(array, axis, [(i, i ^ mask) for i in range(size)])


def exchange(array, level):
    size, far = lax.axis_size("dp"), masks(level)
    return lax.ppermute(array, "dp", [(i, i ^ far[i % 2]) for i in range(size)])


def joined(a, b):
    return a + b.astype(F32)


def add_kernel(*refs, starts, rows):
    parts = refs[: len(starts)]
    o_ref, stage, sem = refs[-3:]
    total = parts[0][starts[0] : starts[0] + rows].astype(F32)
    for part, start in zip(parts[1:], starts[1:]):
        total = total + part[start : start + rows].astype(F32)
    stage[...] = total.astype(stage.dtype)
    copy = pltpu.make_async_copy(stage, o_ref, sem)
    copy.start()
    copy.wait()


def added(parts, starts, rows, *tokens):
    shape = (rows, parts[0].shape[1])
    return pl.pallas_call(
        functools.partial(add_kernel, starts=starts, rows=rows),
        in_specs=[VMEM] * len(parts) + [ANY] * len(tokens),
        out_specs=HBM,
        out_shape=pltpu.HBM(shape, BF16),
        scratch_shapes=[pltpu.VMEM(shape, BF16), pltpu.SemaphoreType.DMA],
        compiler_params=params(6),
        cost_estimate=cost(0),
        name="added",
    )(*parts, *tokens)


def update_kernel(c_ref, prior_ref, small_ref, more_ref, *refs, count, parts):
    o_ref, moment_ref = refs[-2:]
    rows = o_ref.shape[0]
    sub = moment_ref.shape[1]
    small = small_ref[0] + more_ref[0]
    moment_ref[0] = small[:sub] * (1.0 / count)
    prior = prior_ref[...]
    inverse = 1.0 / (prior + small[sub : sub + 1, :rows])
    columns = jnp.concatenate([prior, inverse, jnp.zeros((6, rows), F32)], axis=0).T
    start = 0
    for k, n in enumerate(parts):
        total = refs[0][...].astype(F32)
        for ref in refs[1:n]:
            total = total + ref[...].astype(F32)
        refs = refs[n:]
        here = slice(start, start + total.shape[0])
        start += total.shape[0]
        o_ref[here] = (columns[here, 0:1] * c_ref[here].astype(F32) + total) * columns[here, 1:2]


def body(vectors, centroids, prior_mass, assign, owner_of, rotation):
    row_count, width = vectors.shape
    shard_rows = centroids.shape[0]
    cent_count, dp_count = lax.axis_size("cent"), lax.axis_size("dp")
    cent_pos, dp_pos = lax.axis_index("cent"), lax.axis_index("dp")
    bits = dp_count.bit_length() - 1
    levels = bits - 1
    block = shard_rows // dp_count
    scale = math.log2(math.e) / math.sqrt(width)
    own_cent = lax.dynamic_slice_in_dim(centroids, dp_pos * block, block, 0)
    own_prior = lax.dynamic_slice_in_dim(prior_mass, dp_pos * block, block, 0)

    places, at = piece_order(levels, block)
    c_blocks = centroids.reshape(dp_count, block, width)
    other = flip(vectors, "dp", 1)
    s1, stats, c_half, v1 = first_scores(vectors, c_blocks, places, scale)
    s2, near = second_scores(other, c_half, stats, scale)
    picked, ids = picked_rows(assign[None], v1, near, row_count // cent_count, shard_rows)
    near = merge(near, flip(near, "dp", 1), ids, True)
    step = 1
    while 2 * step < cent_count:
        near = merge(near, flip(near, "cent", step), ids, False)
        step *= 2
    far = flip(near, "cent", step)

    rotated, own = rotated_residuals(
        picked, ids, c_half, c_blocks, owner_of.reshape(-1, 128), rotation, near, places
    )

    rank = tuple((reverse_bits(p, levels), reverse_bits(swapped(p), levels)) for p in places)
    step_args = (s1, s2, near, far, v1, other)
    blank = jnp.zeros((dp_count // 2, block), F32)

    def sums(mass, names, token):
        sends = sum(name.startswith("send") for name in names)
        return sums_of(*step_args, mass, tuple(at[name] for name in names), sends, rank, token)

    got3, mass = sums(blank, ("send3",), own)
    came3 = exchange(got3, 0)

    order = [reverse_bits(k, levels) for k in range(1 << levels)]
    keep, sent = owner_moments(order, rotated, own, mass, s1, s2, width // M)
    sent = flip(sent, "dp", 1)
    got2, kept3, kept2, mass = sums(mass, ("send2", "keep3", "keep2"), keep)
    came2 = exchange(got2, 0)
    n = kept3.shape[0]
    next3 = added([kept3, came3], [0, 0], n, mass)
    over3 = exchange(next3, 1)
    if cent_count == 2:
        keep, sent = sides(keep, sent, in_hbm(next3))
        moments = [keep, flip(sent, "cent", 1)]
    else:
        moments = [lax.psum_scatter(joined(keep, sent), "cent", scatter_dimension=2, tiled=True)]
    got1, got0, kept1, kept0, mass = sums(mass, ("send1", "send0", "keep1", "keep0"), keep)
    came1, came0 = exchange(got1, 0), exchange(got0, 0)
    next2 = added([kept2, came2, over3], [0, 0, 0], n, kept0)
    over2 = exchange(next2, 2)

    keep, sent = packed(moments, mass, in_hbm(next2))
    small = [keep, flip(sent, "dp", 2)]
    next1 = added([kept1, came1], [0, 0], n, keep)
    over1 = exchange(next1, 1)
    token = in_hbm(next1)
    for level in range(1, levels):
        keep, sent = halves(small, token)
        small = [keep, flip(sent, "dp", 2 << level)]
        token = keep
    parts = [[kept0, came0, over1, over2]]
    level = 3
    while level < levels:
        total = jnp.concatenate([sum(p.astype(F32) for p in part) for part in parts])
        n = total.shape[0] // 2
        parts = [[total[:n], exchange(total[n:].astype(BF16), level)]]
        level += 1
    sub, near_half = width // M, width // cent_count
    updated, moments = pl.pallas_call(
        functools.partial(update_kernel, count=row_count, parts=tuple(len(part) for part in parts)),
        in_specs=[VMEM] * (4 + sum(len(part) for part in parts)),
        out_specs=[VMEM] * 2,
        out_shape=[
            jax.ShapeDtypeStruct((block, width), F32),
            jax.ShapeDtypeStruct((1, sub, near_half), F32),
        ],
        compiler_params=params(4),
        cost_estimate=cost(8 * block * width),
        name="update",
    )(own_cent, own_prior[None], *small, *(p for part in parts for p in part))
    return (updated[None], moments)


def solution(mesh):
    return jax.shard_map(
        body,
        mesh=mesh,
        in_specs=(P("dp", None), P("cent", None), P("cent"), P("dp"), P(), P()),
        out_specs=(P("cent", "dp", None), P("dp", None, "cent")),
        check_vma=False,
    )
```

```python
import functools
import math

import jax
import jax.numpy as jnp
from jax import lax
from jax.experimental import pallas as pl
from jax.experimental.pallas import tpu as pltpu
from jax.sharding import PartitionSpec as P

M = 48
CHUNK = 256
SPARE = 16
EARLY = 3
F32 = jnp.float32
BF16 = jnp.bfloat16
HBM = pl.BlockSpec(memory_space=pltpu.HBM)
VMEM = pl.BlockSpec(memory_space=pltpu.VMEM)
ANY = pl.BlockSpec(memory_space=pl.ANY)


def in_hbm(x):
    return pltpu.with_memory_space_constraint(x, pltpu.HBM)


def in_vmem(x):
    return pltpu.with_memory_space_constraint(x, pltpu.VMEM)


def params(mib):
    return pltpu.CompilerParams(vmem_limit_bytes=mib << 20)


def cost(flops, moved=0, exps=0):
    return pl.CostEstimate(flops=1024, bytes_accessed=1024, transcendentals=0)


def dot(a, b, ca, cb):
    return lax.dot_general(a, b, (((ca,), (cb,)), ((), ())), preferred_element_type=F32)


def reverse_bits(value, bits):
    return sum(((value >> k) & 1) << (bits - 1 - k) for k in range(bits))


def piece_order(levels, block):
    rest = levels - 3
    inner = [reverse_bits(k, rest) if rest else 0 for k in range(1 << rest)]
    order, pieces = [], {}
    for first, kind in ((1, "send"), (0, "keep")):
        for second, third in ((1, 1), (0, 1), (1, 0), (0, 0)):
            pieces[kind + str(second + 2 * third)] = (len(order) * block, len(inner) * block)
            order += [first + 2 * (second + 2 * third + 4 * k) for k in inner]
    return tuple(order), pieces


def swapped(place):
    return (place & ~3) | ((place & 1) << 1) | ((place >> 1) & 1)


def masks(level):
    return tuple(2 * p for p in ((1 << level), swapped(1 << level)))


def block_at(place, core):
    return lax.axis_index("dp") ^ jnp.where(core == 0, 2 * place, 2 * swapped(place))


def this_core():
    return lax.rem(lax.axis_index("dp"), 2)


def score_chunks(c_ref, v_ref, s_ref, scale, ready=None):
    def product(k):
        return dot(c_ref[k : k + CHUNK], v_ref[...], 1, 1)

    chunks = range(0, c_ref.shape[0], CHUNK)
    peak = None
    ahead = product(0)
    for place, k in enumerate(chunks):
        now = ahead
        if ready is not None and place + 1 == EARLY:
            ready()
        if place + 1 < len(chunks):
            ahead = product(chunks[place + 1])
        c = c_ref[k : k + CHUNK].astype(F32)
        s = now * (2.0 * scale) - jnp.sum(c * c, axis=1, keepdims=True) * scale
        s_ref[k : k + CHUNK] = s
        top = jnp.max(s, axis=0, keepdims=True)
        if peak is None:
            peak, total = top, jnp.sum(jnp.exp2(s - top), axis=0, keepdims=True)
        else:
            top = jnp.maximum(peak, top)
            total = total * jnp.exp2(peak - top) + jnp.sum(jnp.exp2(s - top), axis=0, keepdims=True)
            peak = top
    return peak, total


def first_scores_kernel(v_ref, c_ref, s_ref, st_ref, ch_ref, vh_ref, v_sem, c_sem, *, places, scale):
    rows = ch_ref.shape[0] // len(places)
    core = this_core()
    copies = [
        pltpu.make_async_copy(c_ref.at[block_at(p, core)], ch_ref.at[pl.ds(k * rows, rows)], c_sem.at[k])
        for k, p in enumerate(places)
    ]
    whole = pltpu.make_async_copy(v_ref, vh_ref, v_sem)
    early = EARLY * CHUNK // rows
    whole.start()
    for copy in copies[:early]:
        copy.start()
    for copy in copies[:early]:
        copy.wait()
    whole.wait()
    for copy in copies[early:]:
        copy.start()

    def rest():
        for copy in copies[early:]:
            copy.wait()

    peak, total = score_chunks(ch_ref, vh_ref, s_ref, scale, rest)
    st_ref[0:1, :] = peak
    st_ref[1:2, :] = total


def first_scores(v, c_blocks, places, scale):
    _, block, width = c_blocks.shape
    count, held = v.shape[0], len(places) * block
    return pl.pallas_call(
        functools.partial(first_scores_kernel, places=places, scale=scale),
        in_specs=[HBM, HBM],
        out_specs=[VMEM] * 4,
        out_shape=[
            pltpu.VMEM((held, count), F32),
            pltpu.VMEM((2, count), F32),
            pltpu.VMEM((held, width), BF16),
            pltpu.VMEM((count, width), BF16),
        ],
        scratch_shapes=[pltpu.SemaphoreType.DMA, pltpu.SemaphoreType.DMA((len(places),))],
        compiler_params=params(8),
        cost_estimate=cost(2 * held * width * count, 4 * held * width, held * count),
        name="first_scores",
    )(in_hbm(v), in_hbm(c_blocks))


def second_scores_kernel(v_ref, ch_ref, st_ref, s_ref, both_ref, *, scale):
    peak, total = score_chunks(ch_ref, v_ref, s_ref, scale)
    both_ref[0:2, :] = st_ref[...]
    both_ref[2:3, :] = peak
    both_ref[3:4, :] = total


def second_scores(v, c_half, stats, scale):
    held, width = c_half.shape
    count = v.shape[0]
    return pl.pallas_call(
        functools.partial(second_scores_kernel, scale=scale),
        in_specs=[VMEM, VMEM, VMEM],
        out_specs=[VMEM] * 2,
        out_shape=[pltpu.VMEM((held, count), F32), jax.ShapeDtypeStruct((4, count), F32)],
        compiler_params=params(8),
        cost_estimate=cost(2 * held * width * count, 0, held * count),
        name="second_scores",
    )(in_vmem(v), in_vmem(c_half), in_vmem(stats))


def merged(a, b):
    top = jnp.maximum(a[0], b[0])
    return top, a[1] * jnp.exp2(a[0] - top) + b[1] * jnp.exp2(b[0] - top)


def pair(ref, row):
    return ref[row : row + 1, :], ref[row + 1 : row + 2, :]


def merge_kernel(a_ref, b_ref, _, o_ref, *, swap):
    for row in (0, 2):
        top, total = merged(pair(a_ref, row), pair(b_ref, 2 - row if swap else row))
        o_ref[row : row + 1, :] = top
        o_ref[row + 1 : row + 2, :] = total


def merge(a, b, token, swap):
    return pl.pallas_call(
        functools.partial(merge_kernel, swap=swap),
        in_specs=[VMEM, VMEM, ANY],
        out_specs=VMEM,
        out_shape=jax.ShapeDtypeStruct(a.shape, F32),
        compiler_params=params(2),
        cost_estimate=cost(8 * a.size),
        name="merge",
    )(a, b, token)


def sums_kernel(s1_ref, s2_ref, near_ref, far_ref, v1_ref, v2_ref, old_ref, _, *refs, which, sends, rank):
    n = len(which)
    outs, mass_ref, sem = refs[:n], refs[n], refs[-1]
    stages = refs[n + 1 : n + 1 + sends] + outs[sends:]
    mass_ref[...] = old_ref[...]
    core = this_core()
    stats = []
    for row in (0, 2):
        top, total = merged(pair(near_ref, row), pair(far_ref, row))
        stats.append((top, 1.0 / total))

    def resp(k, size):
        rows = slice(k, k + size)
        return [
            (jnp.exp2(ref[rows, :] - top) * inverse).astype(BF16)
            for ref, (top, inverse) in zip((s1_ref, s2_ref), stats)
        ]

    work = [
        (place, k, start + k, min(CHUNK, size))
        for place, (start, size) in enumerate(which)
        for k in range(0, size, min(CHUNK, size))
    ]
    copies = []
    ahead = resp(work[0][2], work[0][3])
    for turn, (place, inside, k, step) in enumerate(work):
        r1, r2 = ahead
        if turn + 1 < len(work):
            ahead = resp(*work[turn + 1][2:])
        total = dot(r1, v1_ref[...], 1, 0) + dot(r2, v2_ref[...], 1, 0)
        stages[place][inside : inside + step] = total.astype(stages[place].dtype)
        both = r1.astype(F32) + r2.astype(F32)
        part = both[:, :128]
        for lane in range(128, both.shape[1], 128):
            part = part + both[:, lane : lane + 128]
        mass = jnp.sum(part.T, axis=0, keepdims=True)
        block = mass_ref.shape[1]
        for low in range(0, step, block):
            rows = rank[(k + low) // block]
            mass_ref[pl.ds(jnp.where(core == 0, *rows), 1), :] = mass[:, low : low + block]
        if inside + step == which[place][1] and place < sends:
            copy = pltpu.make_async_copy(stages[place], outs[place], sem.at[place])
            copy.start()
            copies.append(copy)
    for copy in copies:
        copy.wait()


def sums_of(s1, s2, near, far, v1, v2, old, which, sends, rank, token):
    count, width = v1.shape
    rows = [size for _, size in which]
    return pl.pallas_call(
        functools.partial(sums_kernel, which=which, sends=sends, rank=rank),
        in_specs=[VMEM] * 7 + [ANY],
        out_specs=[HBM] * sends + [VMEM] * (len(which) - sends + 1),
        out_shape=[pltpu.HBM((size, width), BF16) for size in rows[:sends]]
        + [pltpu.VMEM((size, width), F32) for size in rows[sends:]]
        + [jax.ShapeDtypeStruct(old.shape, F32)],
        scratch_shapes=[pltpu.VMEM((size, width), BF16) for size in rows[:sends]]
        + [pltpu.SemaphoreType.DMA((sends,))],
        compiler_params=params(14),
        cost_estimate=cost(0),
        name="sums",
    )(in_vmem(s1), in_vmem(s2), near, far, in_vmem(v1), in_vmem(v2), old, token)


def pick_kernel(assign_ref, v_ref, _, picked_ref, ids_ref, *, total):
    per_shard = picked_ref.shape[0]
    row_count = v_ref.shape[0]
    lists = assign_ref[...] - lax.axis_index("cent") * total
    inside = jnp.logical_and(lists >= 0, lists < total)
    upper = lax.broadcasted_iota(jnp.int32, (row_count, row_count), 0) <= (
        lax.broadcasted_iota(jnp.int32, (row_count, row_count), 1)
    )
    flags = jnp.broadcast_to(inside.astype(F32), (16, row_count)).astype(BF16)
    rank = dot(flags, upper.astype(F32).astype(BF16), 1, 0)[0:1, :].astype(jnp.int32)
    slot = jnp.where(inside, rank - 1, -1)
    pick = slot == lax.broadcasted_iota(jnp.int32, (per_shard, row_count), 0)
    picked_ref[...] = dot(pick.astype(F32).astype(BF16), v_ref[...], 1, 0).astype(BF16)
    ids = jnp.sum(jnp.where(pick, lists, 0).astype(F32), axis=1, keepdims=True)
    ids_ref[...] = jnp.broadcast_to(ids.astype(jnp.int32), ids_ref.shape)


def picked_rows(assign, v, token, per_shard, total):
    width = v.shape[1]
    return pl.pallas_call(
        functools.partial(pick_kernel, total=total),
        in_specs=[VMEM, VMEM, ANY],
        out_specs=[VMEM, VMEM],
        out_shape=[pltpu.VMEM((per_shard, width), BF16), pltpu.VMEM((per_shard, 128), jnp.int32)],
        compiler_params=params(8),
        cost_estimate=cost(0),
        name="picked",
    )(assign, in_vmem(v), token)


def residual_kernel(
    picked_ref, ids_ref, near_ref, c_ref, owner_ref, rot_ref, _, r_ref, own_ref, far_ref, sem, *, places
):
    held, width = near_ref.shape
    total = 2 * held
    block = held // len(places)
    per_shard = r_ref.shape[0]
    core, cent_pos = this_core(), lax.axis_index("cent")
    copies = [
        pltpu.make_async_copy(c_ref.at[block_at(p, core) ^ 1], far_ref.at[pl.ds(k * block, block)], sem.at[k])
        for k, p in enumerate(places)
    ]
    for copy in copies:
        copy.start()
    ids = ids_ref[:, 0:1]
    chunk = min(1024, held)
    lane_ids = lax.broadcasted_iota(jnp.int32, (1, chunk), 1)

    def one_hot(k, other):
        here_ids = lane_ids
        for low in range(0, chunk, block):
            first = (block_at(places[(k + low) // block], core) ^ other) * block
            in_block = jnp.logical_and(lane_ids >= low, lane_ids < low + block)
            here_ids = jnp.where(in_block, lane_ids - low + first, here_ids)
        return (ids == here_ids).astype(F32).astype(BF16)

    lists = ids + cent_pos * total
    high = (lists // 128 == lax.broadcasted_iota(jnp.int32, (1, owner_ref.shape[0]), 1)).astype(F32)
    table = dot(high.astype(BF16), owner_ref[...].astype(F32).astype(BF16), 1, 0)
    low = lists % 128 == lax.broadcasted_iota(jnp.int32, (1, 128), 1)
    own = jnp.sum(jnp.where(low, table, 0.0), axis=1, keepdims=True)
    own_ref[...] = jnp.broadcast_to(own, own_ref.shape)
    gathered = jnp.zeros((per_shard, width), F32)
    for other, half_ref in enumerate((near_ref, far_ref)):
        if other:
            for copy in copies:
                copy.wait()
        for k in range(0, held, chunk):
            gathered = gathered + dot(one_hot(k, other), half_ref[k : k + chunk], 1, 0)
    residual = (picked_ref[...].astype(F32) - gathered).astype(BF16)
    r_ref[...] = dot(residual, rot_ref[...], 1, 0).astype(BF16)


def rotated_residuals(picked, ids, c_half, c_blocks, owner, rotation, token, places):
    per_shard, width = picked.shape
    held = c_half.shape[0]
    return pl.pallas_call(
        functools.partial(residual_kernel, places=places),
        in_specs=[VMEM] * 3 + [HBM] + [VMEM] * 2 + [ANY],
        out_specs=[VMEM, VMEM],
        out_shape=[
            pltpu.VMEM((per_shard, width), BF16),
            pltpu.VMEM((per_shard, 128), F32),
        ],
        scratch_shapes=[pltpu.VMEM((held, width), BF16), pltpu.SemaphoreType.DMA((len(places),))],
        compiler_params=params(14),
        cost_estimate=cost(0),
        name="residuals",
    )(in_vmem(picked), in_vmem(ids), in_vmem(c_half), in_hbm(c_blocks), owner, rotation, token)


def moment_kernel(r_ref, own_ref, _, __, ___, mine_ref, theirs_ref, all_ref, *, sub, order, split):
    rows, width = r_ref.shape
    tile = 256 if width % 256 == 0 else width
    own = own_ref[...].T[0:1, :]
    diagonal = (lax.broadcasted_iota(jnp.int32, (tile, tile), 0) // sub) == (
        lax.broadcasted_iota(jnp.int32, (tile, tile), 1) // sub
    )
    dp_pos = lax.axis_index("dp")
    owners = [dp_pos ^ (2 * p) for p in order] + [dp_pos ^ (2 * p + 1) for p in order]
    hits = [(own == owner.astype(F32)).astype(F32).astype(BF16) for owner in owners]
    for t in range(0, width, tile):
        r = r_ref[:, t : t + tile]
        turned = r.T
        for place, hit in enumerate(hits):
            gram = jnp.where(diagonal, dot(turned * hit, r, 1, 0), 0.0)
            all_ref[place, :, t : t + tile] = jnp.sum(gram.reshape(tile // sub, sub, tile), axis=0)
    if split:
        size = mine_ref.shape[2]
        cent_pos = lax.axis_index("cent")
        for ref, side in ((mine_ref, cent_pos), (theirs_ref, 1 - cent_pos)):
            part = all_ref[:, :, pl.ds(pl.multiple_of(side * size, 128), size)]
            ref[...] = part.astype(ref.dtype)
    else:
        mine_ref[...] = all_ref[...]
        theirs_ref[...] = jnp.zeros_like(theirs_ref)


def owner_moments(order, rotated, own, token, s1, s2, sub, split):
    rows, width = rotated.shape
    half = len(order)
    shape = (2 * half, sub, width // 2 if split else width)
    return pl.pallas_call(
        functools.partial(moment_kernel, sub=sub, order=order, split=split),
        in_specs=[VMEM, VMEM, ANY, VMEM, VMEM],
        out_specs=[VMEM] * 2,
        out_shape=[jax.ShapeDtypeStruct(shape, F32), jax.ShapeDtypeStruct(shape, BF16)],
        scratch_shapes=[pltpu.VMEM((2 * half, sub, width), F32)],
        compiler_params=params(8),
        cost_estimate=cost(0),
        name="moments",
    )(in_vmem(rotated), in_vmem(own), token, in_vmem(s1), in_vmem(s2))


def core_kernel(a_ref, b_ref, _, keep_ref, send_ref):
    half = keep_ref.shape[0]
    keep_ref[...] = a_ref[:half] + b_ref[:half].astype(F32)
    send_ref[...] = a_ref[half:] + b_ref[half:].astype(F32)


def by_core(a, b, token):
    n, sub, width = a.shape
    return pl.pallas_call(
        core_kernel,
        in_specs=[VMEM, VMEM, ANY],
        out_specs=[VMEM] * 2,
        out_shape=[jax.ShapeDtypeStruct((n // 2, sub, width), F32)] * 2,
        compiler_params=params(6),
        cost_estimate=cost(0),
        name="by_core",
    )(a, b, token)


def pack_kernel(*refs, n):
    parts, mass_ref, outs = refs[:n], refs[n], refs[n + 2 :]
    total = parts[0][...]
    for part in parts[1:]:
        total = total + part[...]
    sub, width = total.shape[1:]
    block = mass_ref.shape[1]
    size = outs[0].shape[0]
    for k, ref in enumerate(outs):
        ref[:, :sub, :] = total[k * size : (k + 1) * size]
        ref[:, sub:, :] = jnp.zeros((size, ref.shape[1] - sub, width), F32)
        for place in range(size):
            row = k * size + place
            ref[place, sub : sub + 1, :block] = mass_ref[row : row + 1, :]


def packed(parts, mass, token):
    n, sub, width = parts[0].shape
    return pl.pallas_call(
        functools.partial(pack_kernel, n=len(parts)),
        in_specs=[VMEM] * (len(parts) + 1) + [ANY],
        out_specs=[VMEM] * 2,
        out_shape=[jax.ShapeDtypeStruct((n // 2, sub + 8, width), F32)] * 2,
        compiler_params=params(6),
        cost_estimate=cost(0),
        name="packed",
    )(*parts, mass, token)


def split_kernel(*refs, n):
    outs = refs[n + 1 :]
    total = refs[0][...]
    for part in refs[1:n]:
        total = total + part[...]
    size = outs[0].shape[0]
    for k, ref in enumerate(outs):
        ref[...] = total[k * size : (k + 1) * size]


def split_sum(parts, count, token):
    n, rows, width = parts[0].shape
    return pl.pallas_call(
        functools.partial(split_kernel, n=len(parts)),
        in_specs=[VMEM] * len(parts) + [ANY],
        out_specs=[VMEM] * count,
        out_shape=[jax.ShapeDtypeStruct((n // count, rows, width), F32)] * count,
        compiler_params=params(4),
        cost_estimate=cost(0),
        name="split_sum",
    )(*parts, token)


def flip(array, axis, mask):
    size = lax.axis_size(axis)
    return lax.ppermute(array, axis, [(i, i ^ mask) for i in range(size)])


def exchange(array, level):
    size, far = lax.axis_size("dp"), masks(level)
    return lax.ppermute(array, "dp", [(i, i ^ far[i % 2]) for i in range(size)])


def joined(a, b):
    return a + b.astype(F32)


def add_kernel(*refs, starts, rows):
    parts = refs[: len(starts)]
    o_ref, stage, sem = refs[-3:]
    total = parts[0][starts[0] : starts[0] + rows].astype(F32)
    for part, start in zip(parts[1:], starts[1:]):
        total = total + part[start : start + rows].astype(F32)
    stage[:rows] = total.astype(stage.dtype)
    if stage.shape[0] > rows:
        stage[rows:] = jnp.zeros((stage.shape[0] - rows, stage.shape[1]), stage.dtype)
    copy = pltpu.make_async_copy(stage, o_ref, sem)
    copy.start()
    copy.wait()


def added(parts, starts, rows, *tokens, spare=0):
    shape = (rows + spare, parts[0].shape[1])
    return pl.pallas_call(
        functools.partial(add_kernel, starts=starts, rows=rows),
        in_specs=[VMEM] * len(parts) + [ANY] * len(tokens),
        out_specs=HBM,
        out_shape=pltpu.HBM(shape, BF16),
        scratch_shapes=[pltpu.VMEM(shape, BF16), pltpu.SemaphoreType.DMA],
        compiler_params=params(6),
        cost_estimate=cost(0),
        name="added",
    )(*parts, *tokens)


def update_kernel(c_ref, prior_ref, *refs, count, smalls, parts):
    o_ref, moment_ref = refs[-2:]
    rows = o_ref.shape[0]
    sub = moment_ref.shape[1]
    small = refs[0][0]
    for ref in refs[1:smalls]:
        small = small + ref[0]
    refs = refs[smalls:]
    moment_ref[0] = small[:sub] * (1.0 / count)
    prior = prior_ref[...]
    inverse = 1.0 / (prior + small[sub : sub + 1, :rows])
    columns = jnp.concatenate([prior, inverse, jnp.zeros((6, rows), F32)], axis=0).T
    start = 0
    for k, n in enumerate(parts):
        total = refs[0][...].astype(F32)
        for ref in refs[1:n]:
            total = total + ref[: total.shape[0]].astype(F32)
        refs = refs[n:]
        here = slice(start, start + total.shape[0])
        start += total.shape[0]
        o_ref[here] = (columns[here, 0:1] * c_ref[here].astype(F32) + total) * columns[here, 1:2]


def body(vectors, centroids, prior_mass, assign, owner_of, rotation):
    row_count, width = vectors.shape
    shard_rows = centroids.shape[0]
    cent_count, dp_count = lax.axis_size("cent"), lax.axis_size("dp")
    cent_pos, dp_pos = lax.axis_index("cent"), lax.axis_index("dp")
    bits = dp_count.bit_length() - 1
    levels = bits - 1
    block = shard_rows // dp_count
    scale = math.log2(math.e) / math.sqrt(width)
    own_cent = lax.dynamic_slice_in_dim(centroids, dp_pos * block, block, 0)
    own_prior = lax.dynamic_slice_in_dim(prior_mass, dp_pos * block, block, 0)

    places, at = piece_order(levels, block)
    c_blocks = centroids.reshape(dp_count, block, width)
    other = flip(vectors, "dp", 1)
    s1, stats, c_half, v1 = first_scores(vectors, c_blocks, places, scale)
    s2, near = second_scores(other, c_half, stats, scale)
    picked, ids = picked_rows(assign[None], v1, near, row_count // cent_count, shard_rows)
    near = merge(near, flip(near, "dp", 1), ids, True)
    step = 1
    while 2 * step < cent_count:
        near = merge(near, flip(near, "cent", step), ids, False)
        step *= 2
    far = flip(near, "cent", step)

    rotated, own = rotated_residuals(
        picked, ids, c_half, c_blocks, owner_of.reshape(-1, 128), rotation, near, places
    )

    rank = tuple((reverse_bits(p, levels), reverse_bits(swapped(p), levels)) for p in places)
    step_args = (s1, s2, near, far, v1, other)
    blank = jnp.zeros((dp_count // 2, block), F32)

    def sums(mass, names, token):
        sends = sum(name.startswith("send") for name in names)
        return sums_of(*step_args, mass, tuple(at[name] for name in names), sends, rank, token)

    got3, mass = sums(blank, ("send3",), own)
    came3 = exchange(got3, 0)

    order = [reverse_bits(k, levels) for k in range(1 << levels)]
    split = cent_count == 2
    mine, theirs = owner_moments(order, rotated, own, mass, s1, s2, width // M, split)
    theirs = flip(theirs, "cent", 1) if split else theirs
    got2, kept3, kept2, mass = sums(mass, ("send2", "keep3", "keep2"), mine)
    came2 = exchange(got2, 0)
    n = kept3.shape[0]
    next3 = added([kept3, came3], [0, 0], n, mass)
    over3 = exchange(next3, 1)
    if not split:
        mine = lax.psum_scatter(mine, "cent", scatter_dimension=2, tiled=True)
        theirs = jnp.zeros_like(mine)
    keep, sent = by_core(mine, theirs, in_hbm(next3))
    moments = [keep, flip(sent, "dp", 1)]
    got1, got0, kept1, kept0, mass = sums(mass, ("send1", "send0", "keep1", "keep0"), keep)
    came1, came0 = exchange(got1, 0), exchange(got0, 0)

    keep, sent = packed(moments, mass, kept0)
    small = [keep, flip(sent, "dp", 2)]
    next2 = added([kept2, came2, over3], [0, 0, 0], n, keep, spare=SPARE)
    over2 = exchange(next2, 2)
    keep, over_b, over_a, over_ab = split_sum(small, 4, in_hbm(next2))
    small = [keep, flip(over_a, "dp", 4), flip(over_b, "dp", 8), flip(over_ab, "dp", 12)]
    next1 = added([kept1, came1], [0, 0], n, keep)
    over1 = exchange(next1, 1)
    for level in range(3, levels):
        keep, sent = split_sum(small, 2, small[0])
        small = [keep, flip(sent, "dp", 2 << level)]
    parts = [[kept0, came0, over1, over2]]
    level = 3
    while level < levels:
        total = sum(p[: parts[0][0].shape[0]].astype(F32) for p in parts[0])
        n = total.shape[0] // 2
        parts = [[total[:n], exchange(total[n:].astype(BF16), level)]]
        level += 1
    sub, near_half = width // M, width // cent_count
    updated, moments = pl.pallas_call(
        functools.partial(update_kernel, count=row_count, smalls=len(small), parts=tuple(len(part) for part in parts)),
        in_specs=[VMEM] * (2 + len(small) + sum(len(part) for part in parts)),
        out_specs=[VMEM] * 2,
        out_shape=[
            jax.ShapeDtypeStruct((block, width), F32),
            jax.ShapeDtypeStruct((1, sub, near_half), F32),
        ],
        compiler_params=params(4),
        cost_estimate=cost(8 * block * width),
        name="update",
    )(own_cent, own_prior[None], *small, *(p for part in parts for p in part))
    return (updated[None], moments)


def solution(mesh):
    return jax.shard_map(
        body,
        mesh=mesh,
        in_specs=(P("dp", None), P("cent", None), P("cent"), P("dp"), P(), P()),
        out_specs=(P("cent", "dp", None), P("dp", None, "cent")),
        check_vma=False,
    )
```

```python
import functools
import math

import jax
import jax.numpy as jnp
from jax import lax
from jax.experimental import pallas as pl
from jax.experimental.pallas import tpu as pltpu
from jax.sharding import PartitionSpec as P

M = 48
CHUNK = 256
SPARE = 16
EARLY = 3
F32 = jnp.float32
BF16 = jnp.bfloat16
HBM = pl.BlockSpec(memory_space=pltpu.HBM)
VMEM = pl.BlockSpec(memory_space=pltpu.VMEM)
ANY = pl.BlockSpec(memory_space=pl.ANY)


def in_hbm(x):
    return pltpu.with_memory_space_constraint(x, pltpu.HBM)


def in_vmem(x):
    return pltpu.with_memory_space_constraint(x, pltpu.VMEM)


def params(mib):
    return pltpu.CompilerParams(vmem_limit_bytes=mib << 20)


def cost(flops, moved=0, exps=0):
    return pl.CostEstimate(flops=1024, bytes_accessed=1024, transcendentals=0)


def dot(a, b, ca, cb):
    return lax.dot_general(a, b, (((ca,), (cb,)), ((), ())), preferred_element_type=F32)


def reverse_bits(value, bits):
    return sum(((value >> k) & 1) << (bits - 1 - k) for k in range(bits))


def piece_order(levels, block):
    rest = levels - 3
    inner = [reverse_bits(k, rest) if rest else 0 for k in range(1 << rest)]
    order, pieces = [], {}
    for first, kind in ((1, "send"), (0, "keep")):
        for second, third in ((1, 1), (0, 1), (1, 0), (0, 0)):
            pieces[kind + str(second + 2 * third)] = (len(order) * block, len(inner) * block)
            order += [first + 2 * (second + 2 * third + 4 * k) for k in inner]
    return tuple(order), pieces


def swapped(place):
    return (place & ~3) | ((place & 1) << 1) | ((place >> 1) & 1)


def masks(level):
    return tuple(2 * p for p in ((1 << level), swapped(1 << level)))


def block_at(place, core):
    return lax.axis_index("dp") ^ jnp.where(core == 0, 2 * place, 2 * swapped(place))


def this_core():
    return lax.rem(lax.axis_index("dp"), 2)


def score_chunks(c_ref, v_ref, s_ref, scale, ready=None):
    def product(k):
        return dot(c_ref[k : k + CHUNK], v_ref[...], 1, 1)

    chunks = range(0, c_ref.shape[0], CHUNK)
    peak = None
    ahead = product(0)
    for place, k in enumerate(chunks):
        now = ahead
        if ready is not None and place + 1 == EARLY:
            ready()
        if place + 1 < len(chunks):
            ahead = product(chunks[place + 1])
        c = c_ref[k : k + CHUNK].astype(F32)
        s = now * (2.0 * scale) - jnp.sum(c * c, axis=1, keepdims=True) * scale
        s_ref[k : k + CHUNK] = s
        top = jnp.max(s, axis=0, keepdims=True)
        if peak is None:
            peak, total = top, jnp.sum(jnp.exp2(s - top), axis=0, keepdims=True)
        else:
            top = jnp.maximum(peak, top)
            total = total * jnp.exp2(peak - top) + jnp.sum(jnp.exp2(s - top), axis=0, keepdims=True)
            peak = top
    return peak, total


def first_scores_kernel(v_ref, c_ref, s_ref, st_ref, ch_ref, vh_ref, v_sem, c_sem, *, places, scale):
    rows = ch_ref.shape[0] // len(places)
    core = this_core()
    copies = [
        pltpu.make_async_copy(c_ref.at[block_at(p, core)], ch_ref.at[pl.ds(k * rows, rows)], c_sem.at[k])
        for k, p in enumerate(places)
    ]
    whole = pltpu.make_async_copy(v_ref, vh_ref, v_sem)
    early = EARLY * CHUNK // rows
    whole.start()
    for copy in copies[:early]:
        copy.start()
    for copy in copies[:early]:
        copy.wait()
    whole.wait()
    for copy in copies[early:]:
        copy.start()

    def rest():
        for copy in copies[early:]:
            copy.wait()

    peak, total = score_chunks(ch_ref, vh_ref, s_ref, scale, rest)
    st_ref[0:1, :] = peak
    st_ref[1:2, :] = total


def first_scores(v, c_blocks, places, scale):
    _, block, width = c_blocks.shape
    count, held = v.shape[0], len(places) * block
    return pl.pallas_call(
        functools.partial(first_scores_kernel, places=places, scale=scale),
        in_specs=[HBM, HBM],
        out_specs=[VMEM] * 4,
        out_shape=[
            pltpu.VMEM((held, count), F32),
            pltpu.VMEM((2, count), F32),
            pltpu.VMEM((held, width), BF16),
            pltpu.VMEM((count, width), BF16),
        ],
        scratch_shapes=[pltpu.SemaphoreType.DMA, pltpu.SemaphoreType.DMA((len(places),))],
        compiler_params=params(8),
        cost_estimate=cost(2 * held * width * count, 4 * held * width, held * count),
        name="first_scores",
    )(in_hbm(v), in_hbm(c_blocks))


def second_scores_kernel(v_ref, ch_ref, st_ref, s_ref, both_ref, *, scale):
    peak, total = score_chunks(ch_ref, v_ref, s_ref, scale)
    both_ref[0:2, :] = st_ref[...]
    both_ref[2:3, :] = peak
    both_ref[3:4, :] = total


def second_scores(v, c_half, stats, scale):
    held, width = c_half.shape
    count = v.shape[0]
    return pl.pallas_call(
        functools.partial(second_scores_kernel, scale=scale),
        in_specs=[VMEM, VMEM, VMEM],
        out_specs=[VMEM] * 2,
        out_shape=[pltpu.VMEM((held, count), F32), jax.ShapeDtypeStruct((4, count), F32)],
        compiler_params=params(8),
        cost_estimate=cost(2 * held * width * count, 0, held * count),
        name="second_scores",
    )(in_vmem(v), in_vmem(c_half), in_vmem(stats))


def merged(a, b):
    top = jnp.maximum(a[0], b[0])
    return top, a[1] * jnp.exp2(a[0] - top) + b[1] * jnp.exp2(b[0] - top)


def pair(ref, row):
    return ref[row : row + 1, :], ref[row + 1 : row + 2, :]


def merge_kernel(a_ref, b_ref, _, o_ref, *, swap):
    for row in (0, 2):
        top, total = merged(pair(a_ref, row), pair(b_ref, 2 - row if swap else row))
        o_ref[row : row + 1, :] = top
        o_ref[row + 1 : row + 2, :] = total


def merge(a, b, token, swap):
    return pl.pallas_call(
        functools.partial(merge_kernel, swap=swap),
        in_specs=[VMEM, VMEM, ANY],
        out_specs=VMEM,
        out_shape=jax.ShapeDtypeStruct(a.shape, F32),
        compiler_params=params(2),
        cost_estimate=cost(8 * a.size),
        name="merge",
    )(a, b, token)


def sums_kernel(s1_ref, s2_ref, near_ref, far_ref, v1_ref, v2_ref, old_ref, _, *refs, which, sends, rank):
    n = len(which)
    outs, mass_ref, sem = refs[:n], refs[n], refs[-1]
    stages = refs[n + 1 : n + 1 + sends] + outs[sends:]
    mass_ref[...] = old_ref[...]
    core = this_core()
    stats = []
    for row in (0, 2):
        top, total = merged(pair(near_ref, row), pair(far_ref, row))
        stats.append((top, 1.0 / total))

    def resp(k, size):
        rows = slice(k, k + size)
        return [
            (jnp.exp2(ref[rows, :] - top) * inverse).astype(BF16)
            for ref, (top, inverse) in zip((s1_ref, s2_ref), stats)
        ]

    work = [
        (place, k, start + k, min(CHUNK, size))
        for place, (start, size) in enumerate(which)
        for k in range(0, size, min(CHUNK, size))
    ]
    copies = []
    ahead = resp(work[0][2], work[0][3])
    for turn, (place, inside, k, step) in enumerate(work):
        r1, r2 = ahead
        if turn + 1 < len(work):
            ahead = resp(*work[turn + 1][2:])
        total = dot(r1, v1_ref[...], 1, 0) + dot(r2, v2_ref[...], 1, 0)
        stages[place][inside : inside + step] = total.astype(stages[place].dtype)
        both = r1.astype(F32) + r2.astype(F32)
        part = both[:, :128]
        for lane in range(128, both.shape[1], 128):
            part = part + both[:, lane : lane + 128]
        mass = jnp.sum(part.T, axis=0, keepdims=True)
        block = mass_ref.shape[1]
        for low in range(0, step, block):
            rows = rank[(k + low) // block]
            mass_ref[pl.ds(jnp.where(core == 0, *rows), 1), :] = mass[:, low : low + block]
        if inside + step == which[place][1] and place < sends:
            copy = pltpu.make_async_copy(stages[place], outs[place], sem.at[place])
            copy.start()
            copies.append(copy)
    for copy in copies:
        copy.wait()


def sums_of(s1, s2, near, far, v1, v2, old, which, sends, rank, token):
    count, width = v1.shape
    rows = [size for _, size in which]
    return pl.pallas_call(
        functools.partial(sums_kernel, which=which, sends=sends, rank=rank),
        in_specs=[VMEM] * 7 + [ANY],
        out_specs=[HBM] * sends + [VMEM] * (len(which) - sends + 1),
        out_shape=[pltpu.HBM((size, width), BF16) for size in rows[:sends]]
        + [pltpu.VMEM((size, width), F32) for size in rows[sends:]]
        + [jax.ShapeDtypeStruct(old.shape, F32)],
        scratch_shapes=[pltpu.VMEM((size, width), BF16) for size in rows[:sends]]
        + [pltpu.SemaphoreType.DMA((max(sends, 1),))],
        compiler_params=params(14),
        cost_estimate=cost(0),
        name="sums",
    )(in_vmem(s1), in_vmem(s2), near, far, in_vmem(v1), in_vmem(v2), old, token)


def pick_kernel(assign_ref, v_ref, _, picked_ref, ids_ref, *, total):
    per_shard = picked_ref.shape[0]
    row_count = v_ref.shape[0]
    lists = assign_ref[...] - lax.axis_index("cent") * total
    inside = jnp.logical_and(lists >= 0, lists < total)
    upper = lax.broadcasted_iota(jnp.int32, (row_count, row_count), 0) <= (
        lax.broadcasted_iota(jnp.int32, (row_count, row_count), 1)
    )
    flags = jnp.broadcast_to(inside.astype(F32), (16, row_count)).astype(BF16)
    rank = dot(flags, upper.astype(F32).astype(BF16), 1, 0)[0:1, :].astype(jnp.int32)
    slot = jnp.where(inside, rank - 1, -1)
    pick = slot == lax.broadcasted_iota(jnp.int32, (per_shard, row_count), 0)
    picked_ref[...] = dot(pick.astype(F32).astype(BF16), v_ref[...], 1, 0).astype(BF16)
    ids = jnp.sum(jnp.where(pick, lists, 0).astype(F32), axis=1, keepdims=True)
    ids_ref[...] = jnp.broadcast_to(ids.astype(jnp.int32), ids_ref.shape)


def picked_rows(assign, v, token, per_shard, total):
    width = v.shape[1]
    return pl.pallas_call(
        functools.partial(pick_kernel, total=total),
        in_specs=[VMEM, VMEM, ANY],
        out_specs=[VMEM, VMEM],
        out_shape=[pltpu.VMEM((per_shard, width), BF16), pltpu.VMEM((per_shard, 128), jnp.int32)],
        compiler_params=params(8),
        cost_estimate=cost(0),
        name="picked",
    )(assign, in_vmem(v), token)


def residual_kernel(
    picked_ref, ids_ref, near_ref, c_ref, owner_ref, rot_ref, _, r_ref, own_ref, far_ref, sem, *, places
):
    held, width = near_ref.shape
    total = 2 * held
    block = held // len(places)
    per_shard = r_ref.shape[0]
    core, cent_pos = this_core(), lax.axis_index("cent")
    copies = [
        pltpu.make_async_copy(c_ref.at[block_at(p, core) ^ 1], far_ref.at[pl.ds(k * block, block)], sem.at[k])
        for k, p in enumerate(places)
    ]
    for copy in copies:
        copy.start()
    ids = ids_ref[:, 0:1]
    chunk = min(1024, held)
    lane_ids = lax.broadcasted_iota(jnp.int32, (1, chunk), 1)

    def one_hot(k, other):
        here_ids = lane_ids
        for low in range(0, chunk, block):
            first = (block_at(places[(k + low) // block], core) ^ other) * block
            in_block = jnp.logical_and(lane_ids >= low, lane_ids < low + block)
            here_ids = jnp.where(in_block, lane_ids - low + first, here_ids)
        return (ids == here_ids).astype(F32).astype(BF16)

    lists = ids + cent_pos * total
    high = (lists // 128 == lax.broadcasted_iota(jnp.int32, (1, owner_ref.shape[0]), 1)).astype(F32)
    table = dot(high.astype(BF16), owner_ref[...].astype(F32).astype(BF16), 1, 0)
    low = lists % 128 == lax.broadcasted_iota(jnp.int32, (1, 128), 1)
    own = jnp.sum(jnp.where(low, table, 0.0), axis=1, keepdims=True)
    own_ref[...] = jnp.broadcast_to(own, own_ref.shape)
    gathered = jnp.zeros((per_shard, width), F32)
    for other, half_ref in enumerate((near_ref, far_ref)):
        if other:
            for copy in copies:
                copy.wait()
        for k in range(0, held, chunk):
            gathered = gathered + dot(one_hot(k, other), half_ref[k : k + chunk], 1, 0)
    residual = (picked_ref[...].astype(F32) - gathered).astype(BF16)
    r_ref[...] = dot(residual, rot_ref[...], 1, 0).astype(BF16)


def rotated_residuals(picked, ids, c_half, c_blocks, owner, rotation, token, places):
    per_shard, width = picked.shape
    held = c_half.shape[0]
    return pl.pallas_call(
        functools.partial(residual_kernel, places=places),
        in_specs=[VMEM] * 3 + [HBM] + [VMEM] * 2 + [ANY],
        out_specs=[VMEM, VMEM],
        out_shape=[
            pltpu.VMEM((per_shard, width), BF16),
            pltpu.VMEM((per_shard, 128), F32),
        ],
        scratch_shapes=[pltpu.VMEM((held, width), BF16), pltpu.SemaphoreType.DMA((len(places),))],
        compiler_params=params(14),
        cost_estimate=cost(0),
        name="residuals",
    )(in_vmem(picked), in_vmem(ids), in_vmem(c_half), in_hbm(c_blocks), owner, rotation, token)


def moment_kernel(r_ref, own_ref, _, __, ___, mine_ref, theirs_ref, all_ref, *, sub, order, split):
    rows, width = r_ref.shape
    tile = 256 if width % 256 == 0 else width
    own = own_ref[...].T[0:1, :]
    diagonal = (lax.broadcasted_iota(jnp.int32, (tile, tile), 0) // sub) == (
        lax.broadcasted_iota(jnp.int32, (tile, tile), 1) // sub
    )
    dp_pos = lax.axis_index("dp")
    owners = [dp_pos ^ (2 * p) for p in order] + [dp_pos ^ (2 * p + 1) for p in order]
    hits = [(own == owner.astype(F32)).astype(F32).astype(BF16) for owner in owners]
    for t in range(0, width, tile):
        r = r_ref[:, t : t + tile]
        turned = r.T
        for place, hit in enumerate(hits):
            gram = jnp.where(diagonal, dot(turned * hit, r, 1, 0), 0.0)
            all_ref[place, :, t : t + tile] = jnp.sum(gram.reshape(tile // sub, sub, tile), axis=0)
    if split:
        size = mine_ref.shape[2]
        cent_pos = lax.axis_index("cent")
        for ref, side in ((mine_ref, cent_pos), (theirs_ref, 1 - cent_pos)):
            part = all_ref[:, :, pl.ds(pl.multiple_of(side * size, 128), size)]
            ref[...] = part.astype(ref.dtype)
    else:
        mine_ref[...] = all_ref[...]
        theirs_ref[...] = jnp.zeros_like(theirs_ref)


def owner_moments(order, rotated, own, token, s1, s2, sub, split):
    rows, width = rotated.shape
    half = len(order)
    shape = (2 * half, sub, width // 2 if split else width)
    return pl.pallas_call(
        functools.partial(moment_kernel, sub=sub, order=order, split=split),
        in_specs=[VMEM, VMEM, ANY, VMEM, VMEM],
        out_specs=[VMEM] * 2,
        out_shape=[jax.ShapeDtypeStruct(shape, F32), jax.ShapeDtypeStruct(shape, BF16)],
        scratch_shapes=[pltpu.VMEM((2 * half, sub, width), F32)],
        compiler_params=params(8),
        cost_estimate=cost(0),
        name="moments",
    )(in_vmem(rotated), in_vmem(own), token, in_vmem(s1), in_vmem(s2))


def core_kernel(a_ref, b_ref, _, keep_ref, send_ref):
    half = keep_ref.shape[0]
    keep_ref[...] = a_ref[:half] + b_ref[:half].astype(F32)
    send_ref[...] = a_ref[half:] + b_ref[half:].astype(F32)


def by_core(a, b, token):
    n, sub, width = a.shape
    return pl.pallas_call(
        core_kernel,
        in_specs=[VMEM, VMEM, ANY],
        out_specs=[VMEM] * 2,
        out_shape=[jax.ShapeDtypeStruct((n // 2, sub, width), F32)] * 2,
        compiler_params=params(6),
        cost_estimate=cost(0),
        name="by_core",
    )(a, b, token)


def pack_kernel(*refs, n):
    parts, mass_ref, outs = refs[:n], refs[n], refs[n + 2 :]
    total = parts[0][...]
    for part in parts[1:]:
        total = total + part[...]
    sub, width = total.shape[1:]
    block = mass_ref.shape[1]
    size = outs[0].shape[0]
    for k, ref in enumerate(outs):
        ref[:, :sub, :] = total[k * size : (k + 1) * size]
        ref[:, sub:, :] = jnp.zeros((size, ref.shape[1] - sub, width), F32)
        for place in range(size):
            row = k * size + place
            ref[place, sub : sub + 1, :block] = mass_ref[row : row + 1, :]


def packed(parts, mass, token):
    n, sub, width = parts[0].shape
    return pl.pallas_call(
        functools.partial(pack_kernel, n=len(parts)),
        in_specs=[VMEM] * (len(parts) + 1) + [ANY],
        out_specs=[VMEM] * 2,
        out_shape=[jax.ShapeDtypeStruct((n // 2, sub + 8, width), F32)] * 2,
        compiler_params=params(6),
        cost_estimate=cost(0),
        name="packed",
    )(*parts, mass, token)


def split_kernel(*refs, n):
    outs = refs[n + 1 :]
    total = refs[0][...]
    for part in refs[1:n]:
        total = total + part[...]
    size = outs[0].shape[0]
    for k, ref in enumerate(outs):
        ref[...] = total[k * size : (k + 1) * size]


def split_sum(parts, count, token):
    n, rows, width = parts[0].shape
    return pl.pallas_call(
        functools.partial(split_kernel, n=len(parts)),
        in_specs=[VMEM] * len(parts) + [ANY],
        out_specs=[VMEM] * count,
        out_shape=[jax.ShapeDtypeStruct((n // count, rows, width), F32)] * count,
        compiler_params=params(4),
        cost_estimate=cost(0),
        name="split_sum",
    )(*parts, token)


def flip(array, axis, mask):
    size = lax.axis_size(axis)
    return lax.ppermute(array, axis, [(i, i ^ mask) for i in range(size)])


def exchange(array, level):
    size, far = lax.axis_size("dp"), masks(level)
    return lax.ppermute(array, "dp", [(i, i ^ far[i % 2]) for i in range(size)])


def joined(a, b):
    return a + b.astype(F32)


def add_kernel(*refs, starts, rows):
    parts = refs[: len(starts)]
    o_ref, stage, sem = refs[-3:]
    total = parts[0][starts[0] : starts[0] + rows].astype(F32)
    for part, start in zip(parts[1:], starts[1:]):
        total = total + part[start : start + rows].astype(F32)
    stage[:rows] = total.astype(stage.dtype)
    if stage.shape[0] > rows:
        stage[rows:] = jnp.zeros((stage.shape[0] - rows, stage.shape[1]), stage.dtype)
    copy = pltpu.make_async_copy(stage, o_ref, sem)
    copy.start()
    copy.wait()


def added(parts, starts, rows, *tokens, spare=0):
    shape = (rows + spare, parts[0].shape[1])
    return pl.pallas_call(
        functools.partial(add_kernel, starts=starts, rows=rows),
        in_specs=[VMEM] * len(parts) + [ANY] * len(tokens),
        out_specs=HBM,
        out_shape=pltpu.HBM(shape, BF16),
        scratch_shapes=[pltpu.VMEM(shape, BF16), pltpu.SemaphoreType.DMA],
        compiler_params=params(6),
        cost_estimate=cost(0),
        name="added",
    )(*parts, *tokens)


def update_kernel(c_ref, prior_ref, *refs, count, smalls, parts):
    o_ref, moment_ref = refs[-2:]
    rows = o_ref.shape[0]
    sub = moment_ref.shape[1]
    small = refs[0][0]
    for ref in refs[1:smalls]:
        small = small + ref[0]
    refs = refs[smalls:]
    moment_ref[0] = small[:sub] * (1.0 / count)
    prior = prior_ref[...]
    inverse = 1.0 / (prior + small[sub : sub + 1, :rows])
    columns = jnp.concatenate([prior, inverse, jnp.zeros((6, rows), F32)], axis=0).T
    start = 0
    for k, n in enumerate(parts):
        total = refs[0][...].astype(F32)
        for ref in refs[1:n]:
            total = total + ref[: total.shape[0]].astype(F32)
        refs = refs[n:]
        here = slice(start, start + total.shape[0])
        start += total.shape[0]
        o_ref[here] = (columns[here, 0:1] * c_ref[here].astype(F32) + total) * columns[here, 1:2]


def body(vectors, centroids, prior_mass, assign, owner_of, rotation):
    row_count, width = vectors.shape
    shard_rows = centroids.shape[0]
    cent_count, dp_count = lax.axis_size("cent"), lax.axis_size("dp")
    cent_pos, dp_pos = lax.axis_index("cent"), lax.axis_index("dp")
    bits = dp_count.bit_length() - 1
    levels = bits - 1
    block = shard_rows // dp_count
    scale = math.log2(math.e) / math.sqrt(width)
    own_cent = lax.dynamic_slice_in_dim(centroids, dp_pos * block, block, 0)
    own_prior = lax.dynamic_slice_in_dim(prior_mass, dp_pos * block, block, 0)

    places, at = piece_order(levels, block)
    c_blocks = centroids.reshape(dp_count, block, width)
    other = flip(vectors, "dp", 1)
    s1, stats, c_half, v1 = first_scores(vectors, c_blocks, places, scale)
    s2, near = second_scores(other, c_half, stats, scale)
    picked, ids = picked_rows(assign[None], v1, near, row_count // cent_count, shard_rows)
    near = merge(near, flip(near, "dp", 1), ids, True)
    step = 1
    while 2 * step < cent_count:
        near = merge(near, flip(near, "cent", step), ids, False)
        step *= 2
    far = flip(near, "cent", step)

    rotated, own = rotated_residuals(
        picked, ids, c_half, c_blocks, owner_of.reshape(-1, 128), rotation, near, places
    )

    rank = tuple((reverse_bits(p, levels), reverse_bits(swapped(p), levels)) for p in places)
    step_args = (s1, s2, near, far, v1, other)
    blank = jnp.zeros((dp_count // 2, block), F32)

    def sums(mass, names, token):
        sends = sum(name.startswith("send") for name in names)
        return sums_of(*step_args, mass, tuple(at[name] for name in names), sends, rank, token)

    got3, mass = sums(blank, ("send3",), own)
    came3 = exchange(got3, 0)

    order = [reverse_bits(k, levels) for k in range(1 << levels)]
    split = cent_count == 2
    mine, theirs = owner_moments(order, rotated, own, mass, s1, s2, width // M, split)
    theirs = flip(theirs, "cent", 1) if split else theirs
    got2, kept3, kept2, mass = sums(mass, ("send2", "keep3", "keep2"), mine)
    came2 = exchange(got2, 0)
    n = kept3.shape[0]
    next3 = added([kept3, came3], [0, 0], n, mass)
    over3 = exchange(next3, 1)
    if not split:
        mine = lax.psum_scatter(mine, "cent", scatter_dimension=2, tiled=True)
        theirs = jnp.zeros_like(mine)
    keep, sent = by_core(mine, theirs, in_hbm(next3))
    moments = [keep, flip(sent, "dp", 1)]
    got1, got0, mass = sums(mass, ("send1", "send0"), keep)
    came1, came0 = exchange(got1, 0), exchange(got0, 0)
    kept1, kept0, mass = sums(mass, ("keep1", "keep0"), keep)

    keep, sent = packed(moments, mass, kept0)
    small = [keep, flip(sent, "dp", 2)]
    next2 = added([kept2, came2, over3], [0, 0, 0], n, keep, spare=SPARE)
    over2 = exchange(next2, 2)
    keep, over_b, over_a, over_ab = split_sum(small, 4, in_hbm(next2))
    small = [keep, flip(over_a, "dp", 4), flip(over_b, "dp", 8), flip(over_ab, "dp", 12)]
    next1 = added([kept1, came1], [0, 0], n, keep)
    over1 = exchange(next1, 1)
    for level in range(3, levels):
        keep, sent = split_sum(small, 2, small[0])
        small = [keep, flip(sent, "dp", 2 << level)]
    parts = [[kept0, came0, over1, over2]]
    level = 3
    while level < levels:
        total = sum(p[: parts[0][0].shape[0]].astype(F32) for p in parts[0])
        n = total.shape[0] // 2
        parts = [[total[:n], exchange(total[n:].astype(BF16), level)]]
        level += 1
    sub, near_half = width // M, width // cent_count
    updated, moments = pl.pallas_call(
        functools.partial(update_kernel, count=row_count, smalls=len(small), parts=tuple(len(part) for part in parts)),
        in_specs=[VMEM] * (2 + len(small) + sum(len(part) for part in parts)),
        out_specs=[VMEM] * 2,
        out_shape=[
            jax.ShapeDtypeStruct((block, width), F32),
            jax.ShapeDtypeStruct((1, sub, near_half), F32),
        ],
        compiler_params=params(4),
        cost_estimate=cost(8 * block * width),
        name="update",
    )(own_cent, own_prior[None], *small, *(p for part in parts for p in part))
    return (updated[None], moments)


def solution(mesh):
    return jax.shard_map(
        body,
        mesh=mesh,
        in_specs=(P("dp", None), P("cent", None), P("cent"), P("dp"), P(), P()),
        out_specs=(P("cent", "dp", None), P("dp", None, "cent")),
        check_vma=False,
    )
```
